32 devices in a mesh: grp: 4 (over y, core), dev: 8 (over z, x).
Axes of the slice: x: 2, y: 2, z: 4, core: 2. Of those that a mesh axis runs over, the one named last changes fastest.
Arguments:
- features: bfloat16 [64, 128, 768], P(('grp', 'dev'))
- tile_counts: int32 [64], P(('grp', 'dev')), may hold values from 20 to 120
- projection: bfloat16 [768, 512], replicated, may hold values from -0.21875 to 0.21875
Outputs:
- tile_maxima: float32 [64, 64, 128], P('grp', 'dev')
- chamfer: float32 [64, 64], P('grp', 'dev')
The draws below stay inside these ranges and needn't reach their ends.
All inputs are finite; a program needn't handle non-finite values.
Results may differ from the reference program's by a relative error of at most 0.0014.
Values may be sent and summed in bfloat16 or wider, within the bound.
No kernel may reach another device: no remote copies, remote signals or barrier semaphores. Data moves between devices by JAX's collectives and lax.ppermute only.
A program may use at most 64 MiB of HBM per device.

```python
import jax
import jax.numpy as jnp
from jax import lax

P_SIZE = 128
F = 768
E = 512
SLIDES = 64


def draw_features(key, part):
    key = jax.random.fold_in(key, 11)
    key_base, key_pair, key_mix = jax.random.split(key, 3)
    base = jax.random.normal(key_base, (SLIDES, P_SIZE, F), jnp.float32)
    partner = jax.random.permutation(key_pair, SLIDES)
    mix = jax.random.uniform(key_mix, (SLIDES, 1, 1), jnp.float32, 0.3, 1.2)
    copied = jnp.roll(base[partner], 1, axis=1)
    return jnp.clip(base + mix * copied, -6.0, 6.0).astype(jnp.bfloat16)


def place_ends(values, stream_key, low, largest):
    extent = values.shape
    place = [jax.random.randint(jax.random.fold_in(stream_key, axis), (), 0, extent[axis]) for axis in range(len(extent))]
    values = values.at[tuple(place)].set(low)
    longest = extent.index(max(extent))
    place[longest] = (place[longest] + 1) % extent[longest]
    return values.at[tuple(place)].set(largest)


def normal_values(rng, extent, spread, bound, kind=jnp.bfloat16):
    return jnp.clip(spread * jax.random.normal(rng, extent, jnp.float32), -bound, bound).astype(kind)


def setup_inputs(seed: int = 0) -> dict:
    arg_keys = jax.random.split(jax.random.key(seed), 4)
    features = draw_features(jax.random.fold_in(arg_keys[3], 71), 0)
    tile_counts = place_ends(jax.random.randint(arg_keys[1], (SLIDES,), P_SIZE * 5 // 32, P_SIZE * 15 // 16 + 1), jax.random.fold_in(arg_keys[1], 1), P_SIZE * 5 // 32, (P_SIZE * 15 // 16 + 1) - 1).astype(jnp.int32)
    projection = normal_values(arg_keys[2], (F, E), F ** -0.5, 0.21875)
    return dict(features=features, tile_counts=tile_counts, projection=projection)


def embed_tiles(features, projection):
    count, slots, width = features.shape
    raw = jnp.dot(features.reshape(count * slots, width), projection, preferred_element_type=jnp.float32)
    scale = lax.rsqrt(lax.optimization_barrier(jnp.sum(raw * raw, axis=1, keepdims=True)) + 1e-06)
    return (raw * scale).astype(jnp.bfloat16).reshape(count, slots, -1)

def score_block(rows, row_counts, cols, col_counts):
    slots = rows.shape[1]
    position = jnp.arange(slots, dtype=jnp.int32)
    row_valid = position[None, :] < row_counts[:, None]
    col_valid = position[None, :] < col_counts[:, None]
    score = jnp.einsum('ape,bqe->abpq', rows.astype(jnp.float32), cols.astype(jnp.float32))
    forward = lax.optimization_barrier(jnp.max(jnp.where(col_valid[None, :, None, :], score, -4.0), axis=3))
    forward = jnp.where(row_valid[:, None, :], forward, 0.0)
    back = lax.optimization_barrier(jnp.max(jnp.where(row_valid[:, None, :, None], score, -4.0), axis=2))
    back = jnp.where(col_valid[None, :, :], back, 0.0)
    row_mean = lax.optimization_barrier(jnp.sum(forward, axis=2)) / row_counts[:, None].astype(jnp.float32)
    col_mean = lax.optimization_barrier(jnp.sum(back, axis=2)) / col_counts[None, :].astype(jnp.float32)
    return (forward, 0.5 * (row_mean + col_mean))

def reference(features, tile_counts, projection):
    embed = embed_tiles(features, projection)
    total = embed.shape[0]
    group = 4
    rows = embed.reshape(total // group, group, embed.shape[1], embed.shape[2])
    counts = tile_counts.reshape(total // group, group)

    def one_block(pair):
        return score_block(pair[0], pair[1], embed, tile_counts)
    forward, chamfer = lax.map(one_block, (rows, counts))
    tile_maxima = forward.reshape(total, total, embed.shape[1])
    return (tile_maxima, chamfer.reshape(total, total))
```

```python
import functools

import jax
import jax.numpy as jnp
from jax import lax
from jax.experimental import pallas as pl
from jax.experimental.pallas import tpu as pltpu
from jax.sharding import PartitionSpec as P

USED = 120
CHUNK = 16
TAIL = 8
MAIN = USED - TAIL
MARK = 4.0
VMEM_LIMIT = 40 * 1024 * 1024
NT = (((1,), (1,)), ((), ()))
VMEM = pl.BlockSpec(memory_space=pltpu.VMEM)
HBM = pl.BlockSpec(memory_space=pltpu.HBM)
PARAMS = pltpu.CompilerParams(vmem_limit_bytes=VMEM_LIMIT)


def embed_kernel(features_in, counts_in, projection_in, *refs):
    out_ref, features_ref, counts_ref, projection_ref, sems = refs
    copies = [
        pltpu.make_async_copy(projection_in, projection_ref, sems.at[0]),
        pltpu.make_async_copy(features_in, features_ref, sems.at[1]),
        pltpu.make_async_copy(counts_in, counts_ref, sems.at[2]),
    ]
    for copy in copies:
        copy.start()
    for copy in copies:
        copy.wait()
    slides, slots, _ = features_ref.shape
    tails = []
    for s in range(slides):
        raw = jnp.dot(features_ref[s], projection_ref[...], preferred_element_type=jnp.float32)
        scale = lax.rsqrt(jnp.sum(raw * raw, axis=1, keepdims=True) + 1e-06)
        unit = raw * scale
        slot = lax.broadcasted_iota(jnp.int32, unit.shape, 0)
        lane = lax.broadcasted_iota(jnp.int32, unit.shape, 1)
        filled = slot < counts_ref[s]
        unit = jnp.where(filled, unit, jnp.where(lane == 0, MARK, unit[:1]))
        out_ref[pl.ds(s * MAIN, MAIN), :] = unit[:MAIN].astype(out_ref.dtype)
        tails.append(unit[MAIN:USED])
    out_ref[pl.ds(slides * MAIN, slides * TAIL), :] = jnp.concatenate(tails, axis=0).astype(out_ref.dtype)


def embed_tiles(features, tile_counts, projection):
    slides = features.shape[0]
    width = projection.shape[1]
    return pl.pallas_call(
        embed_kernel,
        out_shape=jax.ShapeDtypeStruct((slides * USED, width), jnp.bfloat16),
        in_specs=[HBM] * 3,
        out_specs=VMEM,
        scratch_shapes=[
            pltpu.VMEM(features.shape, features.dtype),
            pltpu.SMEM(tile_counts.shape, tile_counts.dtype),
            pltpu.VMEM(projection.shape, projection.dtype),
            pltpu.SemaphoreType.DMA((3,)),
        ],
        compiler_params=PARAMS,
        name="embed",
    )(*[pltpu.with_memory_space_constraint(x, pltpu.HBM) for x in (features, tile_counts, projection)])


def marked(part):
    return part[:, :1] > 0.5 * MARK


def count_rows(flags, s, per):
    own = [flags[s * MAIN : (s + 1) * MAIN], flags[per * MAIN + s * TAIL : per * MAIN + (s + 1) * TAIL]]
    return sum(jnp.sum(jnp.where(flag, 0.0, 1.0), axis=0, keepdims=True) for flag in own)


def lay_columns(blocks, labels, per, cols, weight_ref):
    tiles, _, width = cols.shape
    chunks = MAIN // CHUNK
    col_slides = tiles * CHUNK // USED
    span = col_slides * CHUNK
    mine = lax.axis_index("grp")
    lane = lax.broadcasted_iota(jnp.int32, (1, span), 1)
    row = lax.broadcasted_iota(jnp.int32, (CHUNK, width), 0)
    column = lax.broadcasted_iota(jnp.int32, (CHUNK, width), 1)
    counts = jnp.ones((1, span), jnp.float32)
    tail_counts = jnp.ones((1, span // 2), jnp.float32)
    whole = {}
    for (mask, pair, offset), block in zip(labels, blocks):
        for start in range(0, block.shape[0], CHUNK):
            whole.setdefault((mask, pair), {})[offset + start] = block[pl.ds(start, CHUNK), :]
    for (mask, pair), parts in whole.items():
        first = ((mine ^ mask) * 2 + pair) * per
        parts = {start: part.astype(jnp.float32) for start, part in parts.items()}
        flags = jnp.concatenate([marked(parts[start]).astype(jnp.float32) for start in sorted(parts)], axis=0) > 0.5
        tops = [parts[s * MAIN][:1] for s in range(per)]
        for s in range(per):
            count = count_rows(flags, s, per)
            counts = jnp.where(lane // CHUNK == first + s, count, counts)
            tail_counts = jnp.where(lane[:, : span // 2] // TAIL == first + s, count, tail_counts)
        for start, part in parts.items():
            flag = jnp.logical_and(marked(part), column == 0)
            if start < per * MAIN:
                s, k = start // MAIN, start % MAIN // CHUNK
                top, index = tops[s], k * col_slides + first + s
            else:
                s = (start - per * MAIN) // TAIL
                top = jnp.where(row < TAIL, tops[s], tops[s + 1])
                index = chunks * col_slides + (first + s) // 2
            cols[index] = jnp.where(flag, top, part).astype(cols.dtype)
    for k in range(chunks):
        tile = (k * CHUNK + lane % CHUNK).astype(jnp.float32)
        weight_ref[pl.ds(k, 1), :] = jnp.where(tile < counts, 0.5 / counts, 0.0)
    tile = (MAIN + lane % TAIL).astype(jnp.float32)[:, : span // 2]
    weight_ref[pl.ds(chunks, 1), : span // 2] = jnp.where(tile < tail_counts, 0.5 / tail_counts, 0.0)


def unmark(piece, per):
    head = piece[:, :128].astype(jnp.float32)
    flag = marked(head)
    row = lax.broadcasted_iota(jnp.int32, head.shape, 0)
    column = lax.broadcasted_iota(jnp.int32, head.shape, 1)
    top = head[:1]
    for s in range(1, per):
        here = jnp.where(row < per * MAIN, row // MAIN, (row - per * MAIN) // TAIL) == s
        top = jnp.where(here, head[s * MAIN : s * MAIN + 1], top)
    head = jnp.where(jnp.logical_and(flag, column == 0), top, head).astype(piece.dtype)
    return jnp.concatenate([head, piece[:, 128:]], axis=1), [count_rows(flag, s, per) for s in range(per)]


def score_pieces(pieces, cols, weight_ref, per, slots, put):
    tiles, _, width = cols.shape
    chunks = MAIN // CHUNK
    col_slides = tiles * CHUNK // USED
    span = col_slides * CHUNK
    flat = cols[...].reshape(tiles * CHUNK, width)
    tile = lax.broadcasted_iota(jnp.int32, (1, slots), 1)
    lane = lax.broadcasted_iota(jnp.int32, (col_slides, span), 1)
    slide = lax.broadcasted_iota(jnp.int32, (col_slides, span), 0)
    clean = [unmark(piece[...], per) for piece in pieces]
    rows = jnp.concatenate([block for block, _ in clean], axis=0)
    score = lax.dot_general(rows, flat, NT, preferred_element_type=jnp.float32)
    parts = [score[:, k * span : (k + 1) * span] for k in range(chunks)]
    last = score[:, chunks * span :]
    best = functools.reduce(jnp.maximum, parts)
    for t in range(len(pieces) * per):
        base, s = t // per * per * USED, t % per
        spots = (base + s * MAIN, MAIN), (base + per * MAIN + s * TAIL, TAIL)
        count = clean[t // per][1][s]

        def gathered(values):
            own = [values[start : start + size] for start, size in spots]
            return jnp.concatenate([*own, jnp.zeros((slots - USED, values.shape[1]), jnp.float32)], axis=0).T

        def highest(values):
            return functools.reduce(
                jnp.maximum, [jnp.max(values[start : start + size], axis=0, keepdims=True) for start, size in spots]
            )

        mine = jnp.maximum(
            jnp.max(gathered(best).reshape(col_slides, CHUNK, slots), axis=1),
            jnp.max(gathered(last).reshape(col_slides, TAIL, slots), axis=1),
        )
        mine = jnp.where(tile.astype(jnp.float32) < count, mine, 0.0)
        back = functools.reduce(jnp.add, [highest(part) * weight_ref[pl.ds(k, 1), :] for k, part in enumerate(parts)])
        rest = highest(last) * weight_ref[pl.ds(chunks, 1), : span // 2]
        mean = jnp.sum(mine * (0.5 / count), axis=1, keepdims=True)
        mean = mean + jnp.sum(jnp.where(lane // CHUNK == slide, back, 0.0), axis=1, keepdims=True)
        half = slice(0, span // 2)
        mean = mean + jnp.sum(jnp.where(lane[:, half] // TAIL == slide[:, half], rest, 0.0), axis=1, keepdims=True)
        put(t, jnp.where(tile == slots - 1, mean, mine))


def first_kernel(count, labels, per, slots, *refs):
    pieces, blocks, (cols, weight_ref, out_ref) = refs[:count], refs[count:-3], refs[-3:]
    lay_columns(blocks, labels, per, cols, weight_ref)

    def put(t, best):
        out_ref[t] = best

    score_pieces(pieces, cols, weight_ref, per, slots, put)


def first_step(pieces, columns, labels, per, slots):
    count = len(pieces) * per
    rows, width = sum(block.shape[0] for block in columns), columns[0].shape[1]
    col_slides = rows // USED
    return pl.pallas_call(
        functools.partial(first_kernel, len(pieces), labels, per, slots),
        out_shape=(
            jax.ShapeDtypeStruct((rows // CHUNK, CHUNK, width), columns[0].dtype),
            jax.ShapeDtypeStruct((MAIN // CHUNK + 1, col_slides * CHUNK), jnp.float32),
            jax.ShapeDtypeStruct((count, col_slides, slots), jnp.float32),
        ),
        in_specs=[VMEM] * (len(pieces) + len(columns)),
        out_specs=(VMEM,) * 3,
        compiler_params=PARAMS,
        name="first_scores",
    )(*pieces, *columns)


def score_kernel(count, per, slots, *refs):
    pieces, (cols, weight_ref, out_ref) = refs[:count], refs[count:]

    def put(t, best):
        out_ref[t] = best

    score_pieces(pieces, cols, weight_ref, per, slots, put)


def score_step(pieces, cols, weight, per, slots):
    count = len(pieces) * per
    return pl.pallas_call(
        functools.partial(score_kernel, len(pieces), per, slots),
        out_shape=jax.ShapeDtypeStruct((count, cols.shape[0] * CHUNK // USED, slots), jnp.float32),
        in_specs=[VMEM] * (len(pieces) + 2),
        out_specs=VMEM,
        compiler_params=PARAMS,
        name="scores",
    )(*pieces, cols, weight)


def finish_kernel(size, groups, count, per, slots, *refs):
    pieces, (cols, weight_ref), refs = refs[:count], refs[count : count + 2], refs[count + 2 :]
    done, out_ref = refs[:-1], refs[-1]
    wide = out_ref.shape[2]
    block = lax.axis_index("dev") // groups
    first = sum(ref.shape[0] for ref in done)

    def keep(r, best):
        for g in range(groups):
            out_ref[g * (size // groups) + block, r] = best[g * wide : (g + 1) * wide]

    r = 0
    for ref in done:
        for n in range(ref.shape[0]):
            keep(r, ref[n])
            r += 1
    score_pieces(pieces, cols, weight_ref, per, slots, lambda t, best: keep(first + t, best))


def finish_step(pieces, cols, weight, done, size, groups, per, slots):
    count = len(pieces) * per + sum(part.shape[0] for part in done)
    wide = done[0].shape[1] // groups
    operands = [*pieces, cols, weight, *done]
    return pl.pallas_call(
        functools.partial(finish_kernel, size, groups, len(pieces), per, slots),
        out_shape=jax.ShapeDtypeStruct((size, count, wide, slots), jnp.float32),
        in_specs=[VMEM] * len(operands),
        out_specs=VMEM,
        compiler_params=PARAMS,
        name="finish",
    )(*operands)


def gather_kernel(size, groups, rows, parts, best_ref, chamfer_ref):
    slots = best_ref.shape[2]
    per = parts.shape[2] // 2
    first = lax.axis_index("dev") % (size // groups) * groups
    tile = lax.broadcasted_iota(jnp.int32, (1, slots), 1)
    lane = lax.broadcasted_iota(jnp.int32, (per, chamfer_ref.shape[1]), 1)
    means = [jnp.zeros((per, chamfer_ref.shape[1]), jnp.float32)] * groups
    for k in range(groups):
        for r, (mask, s) in enumerate(rows):
            a = ((first + k) ^ mask) * per + s
            part = parts[first + k, r]
            kept = jnp.where(tile < USED, part, 0.0)
            for pair in range(2):
                e = k ^ (2 * pair)
                best_ref[a, pl.ds(e * per, per), :] = kept[pair * per : (pair + 1) * per]
                mean = part[pair * per : (pair + 1) * per, slots - 1 :]
                means[e] = jnp.where(lane == a, mean, means[e])
    for e in range(groups):
        chamfer_ref[pl.ds(e * per, per), :] = means[e]


def gather_results(parts, rows, size, groups):
    _, count, wide, slots = parts.shape
    return pl.pallas_call(
        functools.partial(gather_kernel, size, groups, rows),
        out_shape=(
            jax.ShapeDtypeStruct((2 * count, groups * wide // 2, slots), jnp.float32),
            jax.ShapeDtypeStruct((groups * wide // 2, 2 * count), jnp.float32),
        ),
        in_specs=[VMEM],
        out_specs=(VMEM, VMEM),
        compiler_params=PARAMS,
        name="gather_results",
    )(parts)


def flip(value, axis, mask):
    return lax.ppermute(value, axis, [(i, i ^ mask) for i in range(lax.axis_size(axis))])


def relay_kernel(in_ref, out_ref):
    out_ref[...] = in_ref[...]


def relay(block):
    return pl.pallas_call(
        relay_kernel,
        out_shape=jax.ShapeDtypeStruct(block.shape, block.dtype),
        in_specs=[VMEM],
        out_specs=VMEM,
        compiler_params=PARAMS,
        name="relay",
    )(block)


def split_kernel(in_ref, *outs):
    start = 0
    for out_ref in outs:
        out_ref[...] = in_ref[pl.ds(start, out_ref.shape[0]), :]
        start += out_ref.shape[0]


def split_block(block, count):
    rows, width = block.shape
    ends = [-(-n * rows // (count * CHUNK)) * CHUNK for n in range(count + 1)]
    return pl.pallas_call(
        split_kernel,
        out_shape=[jax.ShapeDtypeStruct((end - start, width), block.dtype) for start, end in zip(ends, ends[1:])],
        in_specs=[VMEM],
        out_specs=[VMEM] * count,
        compiler_params=PARAMS,
        name="split_block",
    )(block)


def on_device(features, tile_counts, projection):
    size, groups = lax.axis_size("dev"), lax.axis_size("grp")
    slots = features.shape[1]
    whole = embed_tiles(features, tile_counts, projection)
    per = features.shape[0]
    mirror, across, beside = flip(whole, "dev", 6), flip(whole, "dev", 1), flip(whole, "dev", 2)
    labels, columns = [(0, 0, 0), (0, 1, 0)], [whole, beside]
    bit = groups // 2
    while bit > 1:
        columns += [flip(block, "grp", bit) for block in columns]
        labels += [(mask ^ bit, pair, 0) for mask, pair, _ in labels]
        bit //= 2
    cut = [2, 2, 2, 4]
    cut = [split_block(block, count) for block, count in zip(columns, cut + [2] * len(columns))]
    mirror, cut[0] = lax.optimization_barrier((mirror, cut[0]))
    swapped = [flip(part, "grp", 1) for part in cut[0]]
    swapped, cut[-1] = lax.optimization_barrier((swapped, cut[-1]))
    across, cut[-2] = lax.optimization_barrier((across, cut[-2]))
    ends = [
        (part, (mask, pair, sum(other.shape[0] for other in parts[:n])))
        for parts, (mask, pair, _) in zip(cut, labels)
        for n, part in enumerate(parts)
    ]
    columns += swapped + [flip(part, "grp", 1) for part, _ in ends[len(swapped) :]]
    labels += [(mask ^ 1, pair, offset) for _, (mask, pair, offset) in ends]
    rows = [(whole, 0), (across, 1), (mirror, 6), (flip(mirror, "dev", 1), 7)]
    bit = 8
    while bit < size:
        rows += [(flip(block, "dev", bit), mask ^ bit) for block, mask in rows]
        bit *= 2
    blocks = [block for block, _ in rows]
    early, late = blocks[:-1], blocks[-1:]
    cols, weight, scored = first_step(early[:3], columns, labels, per, slots)
    done = [scored, *[score_step(early[i : i + 3], cols, weight, per, slots) for i in range(3, len(early), 3)]]
    results = finish_step(late, cols, weight, done, size, groups, per, slots)
    parts = lax.all_to_all(results, "dev", split_axis=0, concat_axis=0, tiled=True)
    names = tuple((mask, s) for _, mask in rows for s in range(per))
    best, chamfer = gather_results(parts, names, size, groups)
    return best, chamfer.T


def solution(mesh):
    return jax.shard_map(
        on_device,
        mesh=mesh,
        in_specs=(P(("grp", "dev"), None, None), P(("grp", "dev")), P()),
        out_specs=(P("grp", "dev", None), P("grp", "dev")),
        check_vma=False,
    )
```

```python
import functools

import jax
import jax.numpy as jnp
from jax import lax
from jax.experimental import pallas as pl
from jax.experimental.pallas import tpu as pltpu
from jax.sharding import PartitionSpec as P

USED = 120
CHUNK = 16
TAIL = 8
MAIN = USED - TAIL
MARK = 128.0
LANES = 128
VMEM_LIMIT = 40 * 1024 * 1024
NT = (((1,), (1,)), ((), ()))
VMEM = pl.BlockSpec(memory_space=pltpu.VMEM)
HBM = pl.BlockSpec(memory_space=pltpu.HBM)
PARAMS = pltpu.CompilerParams(vmem_limit_bytes=VMEM_LIMIT)


def embed_kernel(features_in, counts_in, projection_in, *refs):
    out_ref, features_ref, counts_ref, projection_ref, sems = refs
    copies = [
        pltpu.make_async_copy(projection_in, projection_ref, sems.at[0]),
        pltpu.make_async_copy(features_in, features_ref, sems.at[1]),
        pltpu.make_async_copy(counts_in, counts_ref, sems.at[2]),
    ]
    for copy in copies:
        copy.start()
    for copy in copies:
        copy.wait()
    slides, slots, _ = features_ref.shape
    tails = []
    for s in range(slides):
        raw = jnp.dot(features_ref[s], projection_ref[...], preferred_element_type=jnp.float32)
        scale = lax.rsqrt(jnp.sum(raw * raw, axis=1, keepdims=True) + 1e-06)
        unit = raw * scale
        slot = lax.broadcasted_iota(jnp.int32, unit.shape, 0)
        lane = lax.broadcasted_iota(jnp.int32, unit.shape, 1)
        count = counts_ref[s]
        unit = jnp.where(slot < count, unit, jnp.where(lane == 0, MARK + count.astype(jnp.float32), unit[:1]))
        out_ref[pl.ds(s * MAIN, MAIN), :] = unit[:MAIN].astype(out_ref.dtype)
        tails.append(unit[MAIN:USED])
    out_ref[pl.ds(slides * MAIN, slides * TAIL), :] = jnp.concatenate(tails, axis=0).astype(out_ref.dtype)


def embed_tiles(features, tile_counts, projection):
    slides = features.shape[0]
    width = projection.shape[1]
    return pl.pallas_call(
        embed_kernel,
        out_shape=jax.ShapeDtypeStruct((slides * USED, width), jnp.bfloat16),
        in_specs=[HBM] * 3,
        out_specs=VMEM,
        scratch_shapes=[
            pltpu.VMEM(features.shape, features.dtype),
            pltpu.SMEM(tile_counts.shape, tile_counts.dtype),
            pltpu.VMEM(projection.shape, projection.dtype),
            pltpu.SemaphoreType.DMA((3,)),
        ],
        compiler_params=PARAMS,
        name="embed",
    )(*[pltpu.with_memory_space_constraint(x, pltpu.HBM) for x in (features, tile_counts, projection)])


def slide_count(head, row):
    value = head[row : row + 1, :1]
    return jnp.where(value > 2.0, value - MARK, float(USED))


def unmark(head, top):
    column = lax.broadcasted_iota(jnp.int32, head.shape, 1)
    return jnp.where(jnp.logical_and(column == 0, head > 2.0), top, head)


def lay_columns(blocks, labels, per, cols, weight_ref):
    chunks, col_slides, _, _ = cols.shape
    span = col_slides * CHUNK
    mine = lax.axis_index("grp")
    lane = lax.broadcasted_iota(jnp.int32, (1, span), 1)
    counts = jnp.ones((1, span), jnp.float32)
    whole = {}
    for (mask, pair, offset), block in zip(labels, blocks):
        for start in range(0, block.shape[0], CHUNK):
            whole.setdefault((mask, pair), {})[offset + start] = block, start
    for (mask, pair), parts in whole.items():
        first = ((mine ^ mask) * 2 + pair) * per
        heads = {spot: ref[pl.ds(start, CHUNK), :LANES].astype(jnp.float32) for spot, (ref, start) in parts.items()}
        tops = [heads[s * MAIN][:1] for s in range(per)]
        for spot, (ref, start) in parts.items():
            if spot < per * MAIN:
                s, k = spot // MAIN, spot % MAIN // CHUNK
                cols[k, first + s, :, :LANES] = unmark(heads[spot], tops[s]).astype(cols.dtype)
                cols[k, first + s, :, LANES:] = ref[pl.ds(start, CHUNK), LANES:]
                continue
            tail = ref[pl.ds(start, CHUNK), :].astype(jnp.float32)
            for n in range(CHUNK // TAIL):
                s = (spot - per * MAIN) // TAIL + n
                count = slide_count(heads[spot], (n + 1) * TAIL - 1)
                counts = jnp.where(lane // CHUNK == first + s, count, counts)
                own = tail[n * TAIL : (n + 1) * TAIL]
                own = jnp.concatenate([unmark(own[:, :LANES], tops[s]), own[:, LANES:]], axis=1)
                cols[chunks - 1, first + s] = jnp.concatenate([own, own], axis=0).astype(cols.dtype)
    for k in range(chunks):
        tile = (k * CHUNK + lane % CHUNK).astype(jnp.float32)
        weight_ref[pl.ds(k, 1), :] = jnp.where(tile < counts, 0.5 / counts, 0.0)


def clean_rows(piece, per):
    head = piece[:, :LANES].astype(jnp.float32)
    counts = [slide_count(head, per * MAIN + (s + 1) * TAIL - 1) for s in range(per)]
    parts = [unmark(head[s * MAIN : (s + 1) * MAIN], head[s * MAIN : s * MAIN + 1]) for s in range(per)]
    for s in range(per):
        start = per * MAIN + s * TAIL
        parts.append(unmark(head[start : start + TAIL], head[s * MAIN : s * MAIN + 1]))
    head = jnp.concatenate(parts, axis=0).astype(piece.dtype)
    return jnp.concatenate([head, piece[:, LANES:]], axis=1), counts


def score_pieces(pieces, cols, weight_ref, per, slots, put):
    chunks, col_slides, _, width = cols.shape
    span = col_slides * CHUNK
    flat = cols[...].reshape(chunks * span, width)
    tile = lax.broadcasted_iota(jnp.int32, (1, slots), 1)
    lane = lax.broadcasted_iota(jnp.int32, (col_slides, span), 1)
    slide = lax.broadcasted_iota(jnp.int32, (col_slides, span), 0)
    clean = [clean_rows(piece[...], per) for piece in pieces]
    rows = jnp.concatenate([block for block, _ in clean], axis=0)
    score = lax.dot_general(rows, flat, NT, preferred_element_type=jnp.float32)
    parts = [score[:, k * span : (k + 1) * span] for k in range(chunks)]
    best = functools.reduce(jnp.maximum, parts)
    for t in range(len(pieces) * per):
        base, s = t // per * per * USED, t % per
        spots = (base + s * MAIN, MAIN), (base + per * MAIN + s * TAIL, TAIL)
        count = clean[t // per][1][s]
        mine = [best[start : start + size] for start, size in spots]
        mine = jnp.concatenate([*mine, jnp.zeros((slots - USED, span), jnp.float32)], axis=0).T
        mine = jnp.max(mine.reshape(col_slides, CHUNK, slots), axis=1)
        mine = jnp.where(tile.astype(jnp.float32) < count, mine, 0.0)
        back = []
        for k, part in enumerate(parts):
            highest = [jnp.max(part[start : start + size], axis=0, keepdims=True) for start, size in spots]
            back.append(functools.reduce(jnp.maximum, highest) * weight_ref[pl.ds(k, 1), :])
        back = jnp.where(lane // CHUNK == slide, functools.reduce(jnp.add, back), 0.0)
        mean = jnp.sum(mine * (0.5 / count), axis=1, keepdims=True) + jnp.sum(back, axis=1, keepdims=True)
        put(t, jnp.where(tile == slots - 1, mean, mine))


def first_kernel(count, labels, per, slots, *refs):
    pieces, blocks, (cols, weight_ref, out_ref) = refs[:count], refs[count:-3], refs[-3:]
    lay_columns(blocks, labels, per, cols, weight_ref)

    def put(t, best):
        out_ref[t] = best

    score_pieces(pieces, cols, weight_ref, per, slots, put)


def first_step(pieces, columns, labels, per, slots):
    count = len(pieces) * per
    chunks, width = slots // CHUNK, columns[0].shape[1]
    col_slides = sum(block.shape[0] for block in columns) // USED
    return pl.pallas_call(
        functools.partial(first_kernel, len(pieces), labels, per, slots),
        out_shape=(
            jax.ShapeDtypeStruct((chunks, col_slides, CHUNK, width), columns[0].dtype),
            jax.ShapeDtypeStruct((chunks, col_slides * CHUNK), jnp.float32),
            jax.ShapeDtypeStruct((count, col_slides, slots), jnp.float32),
        ),
        in_specs=[VMEM] * (len(pieces) + len(columns)),
        out_specs=(VMEM,) * 3,
        compiler_params=PARAMS,
        name="first_scores",
    )(*pieces, *columns)


def score_kernel(count, per, slots, *refs):
    pieces, (cols, weight_ref, out_ref) = refs[:count], refs[count:]

    def put(t, best):
        out_ref[t] = best

    score_pieces(pieces, cols, weight_ref, per, slots, put)


def score_step(pieces, cols, weight, per, slots):
    count = len(pieces) * per
    return pl.pallas_call(
        functools.partial(score_kernel, len(pieces), per, slots),
        out_shape=jax.ShapeDtypeStruct((count, cols.shape[1], slots), jnp.float32),
        in_specs=[VMEM] * (len(pieces) + 2),
        out_specs=VMEM,
        compiler_params=PARAMS,
        name="scores",
    )(*pieces, cols, weight)


def finish_kernel(size, groups, count, per, slots, *refs):
    pieces, (cols, weight_ref), refs = refs[:count], refs[count : count + 2], refs[count + 2 :]
    done, out_ref = refs[:-1], refs[-1]
    wide = out_ref.shape[2]
    block = lax.axis_index("dev") // groups
    first = sum(ref.shape[0] for ref in done)

    def keep(r, best):
        for g in range(groups):
            out_ref[g * (size // groups) + block, r] = best[g * wide : (g + 1) * wide]

    r = 0
    for ref in done:
        for n in range(ref.shape[0]):
            keep(r, ref[n])
            r += 1
    score_pieces(pieces, cols, weight_ref, per, slots, lambda t, best: keep(first + t, best))


def finish_step(pieces, cols, weight, done, size, groups, per, slots):
    count = len(pieces) * per + sum(part.shape[0] for part in done)
    wide = done[0].shape[1] // groups
    operands = [*pieces, cols, weight, *done]
    return pl.pallas_call(
        functools.partial(finish_kernel, size, groups, len(pieces), per, slots),
        out_shape=jax.ShapeDtypeStruct((size, count, wide, slots), jnp.float32),
        in_specs=[VMEM] * len(operands),
        out_specs=VMEM,
        compiler_params=PARAMS,
        name="finish",
    )(*operands)


def gather_kernel(size, groups, rows, parts, best_ref, chamfer_ref):
    slots = best_ref.shape[2]
    per = parts.shape[2] // 2
    first = lax.axis_index("dev") % (size // groups) * groups
    tile = lax.broadcasted_iota(jnp.int32, (1, slots), 1)
    lane = lax.broadcasted_iota(jnp.int32, (per, chamfer_ref.shape[1]), 1)
    means = [jnp.zeros((per, chamfer_ref.shape[1]), jnp.float32)] * groups
    for k in range(groups):
        for r, (mask, s) in enumerate(rows):
            a = ((first + k) ^ mask) * per + s
            part = parts[first + k, r]
            kept = jnp.where(tile < USED, part, 0.0)
            for pair in range(2):
                e = k ^ (2 * pair)
                best_ref[a, pl.ds(e * per, per), :] = kept[pair * per : (pair + 1) * per]
                mean = part[pair * per : (pair + 1) * per, slots - 1 :]
                means[e] = jnp.where(lane == a, mean, means[e])
    for e in range(groups):
        chamfer_ref[pl.ds(e * per, per), :] = means[e]


def gather_results(parts, rows, size, groups):
    _, count, wide, slots = parts.shape
    return pl.pallas_call(
        functools.partial(gather_kernel, size, groups, rows),
        out_shape=(
            jax.ShapeDtypeStruct((2 * count, groups * wide // 2, slots), jnp.float32),
            jax.ShapeDtypeStruct((groups * wide // 2, 2 * count), jnp.float32),
        ),
        in_specs=[VMEM],
        out_specs=(VMEM, VMEM),
        compiler_params=PARAMS,
        name="gather_results",
    )(parts)


def flip(value, axis, mask):
    return lax.ppermute(value, axis, [(i, i ^ mask) for i in range(lax.axis_size(axis))])


def relay_kernel(in_ref, out_ref):
    out_ref[...] = in_ref[...]


def relay(block):
    return pl.pallas_call(
        relay_kernel,
        out_shape=jax.ShapeDtypeStruct(block.shape, block.dtype),
        in_specs=[VMEM],
        out_specs=VMEM,
        compiler_params=PARAMS,
        name="relay",
    )(block)


def split_kernel(in_ref, *outs):
    start = 0
    for out_ref in outs:
        out_ref[...] = in_ref[pl.ds(start, out_ref.shape[0]), :]
        start += out_ref.shape[0]


def split_block(block, count):
    rows, width = block.shape
    ends = [-(-n * rows // (count * CHUNK)) * CHUNK for n in range(count + 1)]
    return pl.pallas_call(
        split_kernel,
        out_shape=[jax.ShapeDtypeStruct((end - start, width), block.dtype) for start, end in zip(ends, ends[1:])],
        in_specs=[VMEM],
        out_specs=[VMEM] * count,
        compiler_params=PARAMS,
        name="split_block",
    )(block)


def on_device(features, tile_counts, projection):
    size, groups = lax.axis_size("dev"), lax.axis_size("grp")
    slots = features.shape[1]
    whole = embed_tiles(features, tile_counts, projection)
    per = features.shape[0]
    mirror, across, beside = flip(whole, "dev", 6), flip(whole, "dev", 1), flip(whole, "dev", 2)
    labels, columns = [(0, 0, 0), (0, 1, 0)], [whole, beside]
    bit = groups // 2
    while bit > 1:
        columns += [flip(block, "grp", bit) for block in columns]
        labels += [(mask ^ bit, pair, 0) for mask, pair, _ in labels]
        bit //= 2
    cut = [2, 2, 2, 4]
    cut = [split_block(block, count) for block, count in zip(columns, cut + [2] * len(columns))]
    mirror, cut[0] = lax.optimization_barrier((mirror, cut[0]))
    swapped = [flip(part, "grp", 1) for part in cut[0]]
    swapped, cut[-1] = lax.optimization_barrier((swapped, cut[-1]))
    across, cut[-2] = lax.optimization_barrier((across, cut[-2]))
    ends = [
        (part, (mask, pair, sum(other.shape[0] for other in parts[:n])))
        for parts, (mask, pair, _) in zip(cut, labels)
        for n, part in enumerate(parts)
    ]
    columns += swapped + [flip(part, "grp", 1) for part, _ in ends[len(swapped) :]]
    labels += [(mask ^ 1, pair, offset) for _, (mask, pair, offset) in ends]
    rows = [(whole, 0), (across, 1), (mirror, 6), (flip(mirror, "dev", 1), 7)]
    bit = 8
    while bit < size:
        rows += [(flip(block, "dev", bit), mask ^ bit) for block, mask in rows]
        bit *= 2
    blocks = [block for block, _ in rows]
    early, late = blocks[:-1], blocks[-1:]
    cols, weight, scored = first_step(early[:3], columns, labels, per, slots)
    done = [scored, *[score_step(early[i : i + 3], cols, weight, per, slots) for i in range(3, len(early), 3)]]
    results = finish_step(late, cols, weight, done, size, groups, per, slots)
    parts = lax.all_to_all(results, "dev", split_axis=0, concat_axis=0, tiled=True)
    names = tuple((mask, s) for _, mask in rows for s in range(per))
    best, chamfer = gather_results(parts, names, size, groups)
    return best, chamfer.T


def solution(mesh):
    return jax.shard_map(
        on_device,
        mesh=mesh,
        in_specs=(P(("grp", "dev"), None, None), P(("grp", "dev")), P()),
        out_specs=(P("grp", "dev", None), P("grp", "dev")),
        check_vma=False,
    )
```

```python
import functools

import jax
import jax.numpy as jnp
from jax import lax
from jax.experimental import pallas as pl
from jax.experimental.pallas import tpu as pltpu
from jax.sharding import PartitionSpec as P

USED = 120
CHUNK = 16
TAIL = 8
MAIN = USED - TAIL
MARK = 128.0
LANES = 128
VMEM_LIMIT = 40 * 1024 * 1024
NT = (((1,), (1,)), ((), ()))
VMEM = pl.BlockSpec(memory_space=pltpu.VMEM)
HBM = pl.BlockSpec(memory_space=pltpu.HBM)
PARAMS = pltpu.CompilerParams(vmem_limit_bytes=VMEM_LIMIT)


def embed_kernel(features_in, counts_in, projection_in, *refs):
    out_ref, features_ref, counts_ref, projection_ref, sems = refs
    copies = [
        pltpu.make_async_copy(projection_in, projection_ref, sems.at[0]),
        pltpu.make_async_copy(features_in, features_ref, sems.at[1]),
        pltpu.make_async_copy(counts_in, counts_ref, sems.at[2]),
    ]
    for copy in copies:
        copy.start()
    for copy in copies:
        copy.wait()
    slides, slots, _ = features_ref.shape
    tails = []
    for s in range(slides):
        raw = jnp.dot(features_ref[s], projection_ref[...], preferred_element_type=jnp.float32)
        scale = lax.rsqrt(jnp.sum(raw * raw, axis=1, keepdims=True) + 1e-06)
        unit = raw * scale
        slot = lax.broadcasted_iota(jnp.int32, unit.shape, 0)
        lane = lax.broadcasted_iota(jnp.int32, unit.shape, 1)
        count = counts_ref[s]
        unit = jnp.where(slot < count, unit, jnp.where(lane == 0, MARK + count.astype(jnp.float32), unit[:1]))
        out_ref[pl.ds(s * MAIN, MAIN), :] = unit[:MAIN].astype(out_ref.dtype)
        tails.append(unit[MAIN:USED])
    out_ref[pl.ds(slides * MAIN, slides * TAIL), :] = jnp.concatenate(tails, axis=0).astype(out_ref.dtype)


def embed_tiles(features, tile_counts, projection):
    slides = features.shape[0]
    width = projection.shape[1]
    return pl.pallas_call(
        embed_kernel,
        out_shape=jax.ShapeDtypeStruct((slides * USED, width), jnp.bfloat16),
        in_specs=[HBM] * 3,
        out_specs=VMEM,
        scratch_shapes=[
            pltpu.VMEM(features.shape, features.dtype),
            pltpu.SMEM(tile_counts.shape, tile_counts.dtype),
            pltpu.VMEM(projection.shape, projection.dtype),
            pltpu.SemaphoreType.DMA((3,)),
        ],
        compiler_params=PARAMS,
        name="embed",
    )(*[pltpu.with_memory_space_constraint(x, pltpu.HBM) for x in (features, tile_counts, projection)])


def slide_count(head, row):
    value = head[row : row + 1, :1]
    return jnp.where(value > 2.0, value - MARK, float(USED))


def unmark(head, top):
    column = lax.broadcasted_iota(jnp.int32, head.shape, 1)
    return jnp.where(jnp.logical_and(column == 0, head > 2.0), top, head)


def lay_columns(blocks, labels, per, cols, weight_ref):
    chunks, col_slides, _, _ = cols.shape
    span = col_slides * CHUNK
    mine = lax.axis_index("grp")
    lane = lax.broadcasted_iota(jnp.int32, (1, span), 1)
    counts = jnp.ones((1, span), jnp.float32)
    whole = {}
    for (mask, pair, offset), block in zip(labels, blocks):
        for start in range(0, block.shape[0], CHUNK):
            whole.setdefault((mask, pair), {})[offset + start] = block, start
    for (mask, pair), parts in whole.items():
        first = ((mine ^ mask) * 2 + pair) * per
        heads = {spot: ref[pl.ds(start, CHUNK), :LANES].astype(jnp.float32) for spot, (ref, start) in parts.items()}
        tops = [heads[s * MAIN][:1] for s in range(per)]
        for spot, (ref, start) in parts.items():
            if spot < per * MAIN:
                s, k = spot // MAIN, spot % MAIN // CHUNK
                cols[k, first + s, :, :LANES] = unmark(heads[spot], tops[s]).astype(cols.dtype)
                cols[k, first + s, :, LANES:] = ref[pl.ds(start, CHUNK), LANES:]
                continue
            tail = ref[pl.ds(start, CHUNK), :].astype(jnp.float32)
            for n in range(CHUNK // TAIL):
                s = (spot - per * MAIN) // TAIL + n
                count = slide_count(heads[spot], (n + 1) * TAIL - 1)
                counts = jnp.where(lane // CHUNK == first + s, count, counts)
                own = tail[n * TAIL : (n + 1) * TAIL]
                own = jnp.concatenate([unmark(own[:, :LANES], tops[s]), own[:, LANES:]], axis=1)
                cols[chunks - 1, first + s] = jnp.concatenate([own, own], axis=0).astype(cols.dtype)
    for k in range(chunks):
        tile = (k * CHUNK + lane % CHUNK).astype(jnp.float32)
        weight_ref[pl.ds(k, 1), :] = jnp.where(tile < counts, 0.5 / counts, 0.0)


def clean_rows(piece, per):
    head = piece[:, :LANES].astype(jnp.float32)
    counts = [slide_count(head, per * MAIN + (s + 1) * TAIL - 1) for s in range(per)]
    parts = [unmark(head[s * MAIN : (s + 1) * MAIN], head[s * MAIN : s * MAIN + 1]) for s in range(per)]
    for s in range(per):
        start = per * MAIN + s * TAIL
        parts.append(unmark(head[start : start + TAIL], head[s * MAIN : s * MAIN + 1]))
    head = jnp.concatenate(parts, axis=0).astype(piece.dtype)
    return jnp.concatenate([head, piece[:, LANES:]], axis=1), counts


def score_pieces(pieces, cols, weight_ref, per, slots, put):
    chunks, col_slides, _, width = cols.shape
    span = col_slides * CHUNK
    flat = cols[...].reshape(chunks * span, width)
    tile = lax.broadcasted_iota(jnp.int32, (1, slots), 1)
    lane = lax.broadcasted_iota(jnp.int32, (col_slides, span), 1)
    slide = lax.broadcasted_iota(jnp.int32, (col_slides, span), 0)
    clean = [clean_rows(piece[...], per) for piece in pieces]
    rows = jnp.concatenate([block for block, _ in clean], axis=0)
    score = lax.dot_general(rows, flat, NT, preferred_element_type=jnp.float32)
    parts = [score[:, k * span : (k + 1) * span] for k in range(chunks)]
    best = functools.reduce(jnp.maximum, parts)
    for t in range(len(pieces) * per):
        base, s = t // per * per * USED, t % per
        spots = (base + s * MAIN, MAIN), (base + per * MAIN + s * TAIL, TAIL)
        count = clean[t // per][1][s]
        mine = [best[start : start + size] for start, size in spots]
        mine = jnp.concatenate([*mine, jnp.zeros((slots - USED, span), jnp.float32)], axis=0).T
        mine = jnp.max(mine.reshape(col_slides, CHUNK, slots), axis=1)
        mine = jnp.where(tile.astype(jnp.float32) < count, mine, 0.0)
        back = []
        for k, part in enumerate(parts):
            highest = [jnp.max(part[start : start + size], axis=0, keepdims=True) for start, size in spots]
            back.append(functools.reduce(jnp.maximum, highest) * weight_ref[pl.ds(k, 1), :])
        back = jnp.where(lane // CHUNK == slide, functools.reduce(jnp.add, back), 0.0)
        mean = jnp.sum(mine * (0.5 / count), axis=1, keepdims=True) + jnp.sum(back, axis=1, keepdims=True)
        put(t, jnp.where(tile == slots - 1, mean, mine))


def first_kernel(count, labels, per, slots, *refs):
    pieces, blocks, (cols, weight_ref, out_ref) = refs[:count], refs[count:-3], refs[-3:]
    lay_columns(blocks, labels, per, cols, weight_ref)

    def put(t, best):
        out_ref[t] = best

    score_pieces(pieces, cols, weight_ref, per, slots, put)


def first_step(pieces, columns, labels, per, slots):
    count = len(pieces) * per
    chunks, width = slots // CHUNK, columns[0].shape[1]
    col_slides = sum(block.shape[0] for block in columns) // USED
    return pl.pallas_call(
        functools.partial(first_kernel, len(pieces), labels, per, slots),
        out_shape=(
            jax.ShapeDtypeStruct((chunks, col_slides, CHUNK, width), columns[0].dtype),
            jax.ShapeDtypeStruct((chunks, col_slides * CHUNK), jnp.float32),
            jax.ShapeDtypeStruct((count, col_slides, slots), jnp.float32),
        ),
        in_specs=[VMEM] * (len(pieces) + len(columns)),
        out_specs=(VMEM,) * 3,
        compiler_params=PARAMS,
        name="first_scores",
    )(*pieces, *columns)


def score_kernel(count, per, slots, *refs):
    pieces, (cols, weight_ref, out_ref) = refs[:count], refs[count:]

    def put(t, best):
        out_ref[t] = best

    score_pieces(pieces, cols, weight_ref, per, slots, put)


def score_step(pieces, cols, weight, per, slots):
    count = len(pieces) * per
    return pl.pallas_call(
        functools.partial(score_kernel, len(pieces), per, slots),
        out_shape=jax.ShapeDtypeStruct((count, cols.shape[1], slots), jnp.float32),
        in_specs=[VMEM] * (len(pieces) + 2),
        out_specs=VMEM,
        compiler_params=PARAMS,
        name="scores",
    )(*pieces, cols, weight)


def finish_kernel(size, groups, count, per, slots, *refs):
    pieces, (cols, weight_ref), refs = refs[:count], refs[count : count + 2], refs[count + 2 :]
    done, out_ref = refs[:-1], refs[-1]
    wide = out_ref.shape[2]
    block = lax.axis_index("dev") // groups
    first = sum(ref.shape[0] for ref in done)

    def keep(r, best):
        for g in range(groups):
            out_ref[g * (size // groups) + block, r] = best[g * wide : (g + 1) * wide]

    r = 0
    for ref in done:
        for n in range(ref.shape[0]):
            keep(r, ref[n])
            r += 1
    score_pieces(pieces, cols, weight_ref, per, slots, lambda t, best: keep(first + t, best))


def finish_step(pieces, cols, weight, done, size, groups, per, slots):
    count = len(pieces) * per + sum(part.shape[0] for part in done)
    wide = done[0].shape[1] // groups
    operands = [*pieces, cols, weight, *done]
    return pl.pallas_call(
        functools.partial(finish_kernel, size, groups, len(pieces), per, slots),
        out_shape=jax.ShapeDtypeStruct((size, count, wide, slots), jnp.float32),
        in_specs=[VMEM] * len(operands),
        out_specs=VMEM,
        compiler_params=PARAMS,
        name="finish",
    )(*operands)


def gather_kernel(size, groups, rows, parts, best_ref, chamfer_ref):
    slots = best_ref.shape[2]
    per = parts.shape[2] // 2
    first = lax.axis_index("dev") % (size // groups) * groups
    tile = lax.broadcasted_iota(jnp.int32, (1, slots), 1)
    lane = lax.broadcasted_iota(jnp.int32, (per, chamfer_ref.shape[1]), 1)
    means = [jnp.zeros((per, chamfer_ref.shape[1]), jnp.float32)] * groups
    for k in range(groups):
        for r, (mask, s) in enumerate(rows):
            a = ((first + k) ^ mask) * per + s
            part = parts[first + k, r]
            kept = jnp.where(tile < USED, part, 0.0)
            for pair in range(2):
                e = k ^ (2 * pair)
                best_ref[a, pl.ds(e * per, per), :] = kept[pair * per : (pair + 1) * per]
                mean = part[pair * per : (pair + 1) * per, slots - 1 :]
                means[e] = jnp.where(lane == a, mean, means[e])
    for e in range(groups):
        chamfer_ref[pl.ds(e * per, per), :] = means[e]


def gather_results(parts, rows, size, groups):
    _, count, wide, slots = parts.shape
    return pl.pallas_call(
        functools.partial(gather_kernel, size, groups, rows),
        out_shape=(
            jax.ShapeDtypeStruct((2 * count, groups * wide // 2, slots), jnp.float32),
            jax.ShapeDtypeStruct((groups * wide // 2, 2 * count), jnp.float32),
        ),
        in_specs=[VMEM],
        out_specs=(VMEM, VMEM),
        compiler_params=PARAMS,
        name="gather_results",
    )(parts)


def flip(value, axis, mask):
    return lax.ppermute(value, axis, [(i, i ^ mask) for i in range(lax.axis_size(axis))])


def relay_kernel(in_ref, out_ref):
    out_ref[...] = in_ref[...]


def relay(block):
    return pl.pallas_call(
        relay_kernel,
        out_shape=jax.ShapeDtypeStruct(block.shape, block.dtype),
        in_specs=[VMEM],
        out_specs=VMEM,
        compiler_params=PARAMS,
        name="relay",
    )(block)


def split_kernel(in_ref, *outs):
    start = 0
    for out_ref in outs:
        out_ref[...] = in_ref[pl.ds(start, out_ref.shape[0]), :]
        start += out_ref.shape[0]


def split_block(block, count):
    rows, width = block.shape
    ends = [-(-n * rows // (count * CHUNK)) * CHUNK for n in range(count + 1)]
    return pl.pallas_call(
        split_kernel,
        out_shape=[jax.ShapeDtypeStruct((end - start, width), block.dtype) for start, end in zip(ends, ends[1:])],
        in_specs=[VMEM],
        out_specs=[VMEM] * count,
        compiler_params=PARAMS,
        name="split_block",
    )(block)


def on_device(features, tile_counts, projection):
    size, groups = lax.axis_size("dev"), lax.axis_size("grp")
    slots = features.shape[1]
    whole = embed_tiles(features, tile_counts, projection)
    per = features.shape[0]
    mirror, across, beside = flip(whole, "dev", 6), flip(whole, "dev", 1), flip(whole, "dev", 2)
    labels, columns = [(0, 0, 0), (0, 1, 0)], [whole, beside]
    bit = groups // 2
    while bit > 1:
        columns += [flip(block, "grp", bit) for block in columns]
        labels += [(mask ^ bit, pair, 0) for mask, pair, _ in labels]
        bit //= 2
    cut = [2, 2, 2, 4]
    cut = [split_block(block, count) for block, count in zip(columns, cut + [2] * len(columns))]
    swapped = [flip(part, "grp", 1) for part in cut[0]]
    swapped, cut[-1] = lax.optimization_barrier((swapped, cut[-1]))
    mirror, across, cut[-2] = lax.optimization_barrier((mirror, across, cut[-2]))
    ends = [
        (part, (mask, pair, sum(other.shape[0] for other in parts[:n])))
        for parts, (mask, pair, _) in zip(cut, labels)
        for n, part in enumerate(parts)
    ]
    columns += swapped + [flip(part, "grp", 1) for part, _ in ends[len(swapped) :]]
    labels += [(mask ^ 1, pair, offset) for _, (mask, pair, offset) in ends]
    rows = [(whole, 0), (across, 1), (mirror, 6), (flip(mirror, "dev", 1), 7)]
    bit = 8
    while bit < size:
        rows += [(flip(block, "dev", bit), mask ^ bit) for block, mask in rows]
        bit *= 2
    blocks = [block for block, _ in rows]
    early, late = blocks[:-1], blocks[-1:]
    cols, weight, scored = first_step(early[:3], columns, labels, per, slots)
    done = [scored, *[score_step(early[i : i + 3], cols, weight, per, slots) for i in range(3, len(early), 3)]]
    results = finish_step(late, cols, weight, done, size, groups, per, slots)
    parts = lax.all_to_all(results, "dev", split_axis=0, concat_axis=0, tiled=True)
    names = tuple((mask, s) for _, mask in rows for s in range(per))
    best, chamfer = gather_results(parts, names, size, groups)
    return best, chamfer.T


def solution(mesh):
    return jax.shard_map(
        on_device,
        mesh=mesh,
        in_specs=(P(("grp", "dev"), None, None), P(("grp", "dev")), P()),
        out_specs=(P("grp", "dev", None), P("grp", "dev")),
        check_vma=False,
    )
```

```python
import functools

import jax
import jax.numpy as jnp
from jax import lax
from jax.experimental import pallas as pl
from jax.experimental.pallas import tpu as pltpu
from jax.sharding import PartitionSpec as P

USED = 120
CHUNK = 16
TAIL = 8
MAIN = USED - TAIL
MARK = 128.0
LANES = 128
VMEM_LIMIT = 40 * 1024 * 1024
NT = (((1,), (1,)), ((), ()))
VMEM = pl.BlockSpec(memory_space=pltpu.VMEM)
HBM = pl.BlockSpec(memory_space=pltpu.HBM)
PARAMS = pltpu.CompilerParams(vmem_limit_bytes=VMEM_LIMIT)


def embed_kernel(features_in, counts_in, projection_in, *refs):
    out_ref, features_ref, counts_ref, projection_ref, sems = refs
    copies = [
        pltpu.make_async_copy(projection_in, projection_ref, sems.at[0]),
        pltpu.make_async_copy(features_in, features_ref, sems.at[1]),
        pltpu.make_async_copy(counts_in, counts_ref, sems.at[2]),
    ]
    for copy in copies:
        copy.start()
    for copy in copies:
        copy.wait()
    slides, slots, _ = features_ref.shape
    tails = []
    for s in range(slides):
        raw = jnp.dot(features_ref[s], projection_ref[...], preferred_element_type=jnp.float32)
        scale = lax.rsqrt(jnp.sum(raw * raw, axis=1, keepdims=True) + 1e-06)
        unit = raw * scale
        slot = lax.broadcasted_iota(jnp.int32, unit.shape, 0)
        lane = lax.broadcasted_iota(jnp.int32, unit.shape, 1)
        count = counts_ref[s]
        unit = jnp.where(slot < count, unit, jnp.where(lane == 0, MARK + count.astype(jnp.float32), unit[:1]))
        out_ref[pl.ds(s * MAIN, MAIN), :] = unit[:MAIN].astype(out_ref.dtype)
        tails.append(unit[MAIN:USED])
    out_ref[pl.ds(slides * MAIN, slides * TAIL), :] = jnp.concatenate(tails, axis=0).astype(out_ref.dtype)


def embed_tiles(features, tile_counts, projection):
    slides = features.shape[0]
    width = projection.shape[1]
    return pl.pallas_call(
        embed_kernel,
        out_shape=jax.ShapeDtypeStruct((slides * USED, width), jnp.bfloat16),
        in_specs=[HBM] * 3,
        out_specs=VMEM,
        scratch_shapes=[
            pltpu.VMEM(features.shape, features.dtype),
            pltpu.SMEM(tile_counts.shape, tile_counts.dtype),
            pltpu.VMEM(projection.shape, projection.dtype),
            pltpu.SemaphoreType.DMA((3,)),
        ],
        compiler_params=PARAMS,
        name="embed",
    )(*[pltpu.with_memory_space_constraint(x, pltpu.HBM) for x in (features, tile_counts, projection)])


def slide_count(head, row):
    value = head[row : row + 1, :1]
    return jnp.where(value > 2.0, value - MARK, float(USED))


def unmark(head, top):
    column = lax.broadcasted_iota(jnp.int32, head.shape, 1)
    return jnp.where(jnp.logical_and(column == 0, head > 2.0), top, head)


def lay_columns(blocks, labels, per, cols, weight_ref):
    chunks, col_slides, _, _ = cols.shape
    span = col_slides * CHUNK
    mine = lax.axis_index("grp")
    lane = lax.broadcasted_iota(jnp.int32, (1, span), 1)
    counts = jnp.ones((1, span), jnp.float32)
    whole = {}
    for (mask, pair, offset), block in zip(labels, blocks):
        for start in range(0, block.shape[0], CHUNK):
            whole.setdefault((mask, pair), {})[offset + start] = block, start
    for (mask, pair), parts in whole.items():
        first = ((mine ^ mask) * 2 + pair) * per
        heads = {spot: ref[pl.ds(start, CHUNK), :LANES].astype(jnp.float32) for spot, (ref, start) in parts.items()}
        tops = [heads[s * MAIN][:1] for s in range(per)]
        for spot, (ref, start) in parts.items():
            if spot < per * MAIN:
                s, k = spot // MAIN, spot % MAIN // CHUNK
                cols[k, first + s, :, :LANES] = unmark(heads[spot], tops[s]).astype(cols.dtype)
                cols[k, first + s, :, LANES:] = ref[pl.ds(start, CHUNK), LANES:]
                continue
            tail = ref[pl.ds(start, CHUNK), :].astype(jnp.float32)
            for n in range(CHUNK // TAIL):
                s = (spot - per * MAIN) // TAIL + n
                count = slide_count(heads[spot], (n + 1) * TAIL - 1)
                counts = jnp.where(lane // CHUNK == first + s, count, counts)
                own = tail[n * TAIL : (n + 1) * TAIL]
                own = jnp.concatenate([unmark(own[:, :LANES], tops[s]), own[:, LANES:]], axis=1)
                cols[chunks - 1, first + s] = jnp.concatenate([own, own], axis=0).astype(cols.dtype)
    for k in range(chunks):
        tile = (k * CHUNK + lane % CHUNK).astype(jnp.float32)
        weight_ref[pl.ds(k, 1), :] = jnp.where(tile < counts, 0.5 / counts, 0.0)


def clean_rows(piece, per):
    head = piece[:, :LANES].astype(jnp.float32)
    counts = [slide_count(head, per * MAIN + (s + 1) * TAIL - 1) for s in range(per)]
    parts = [unmark(head[s * MAIN : (s + 1) * MAIN], head[s * MAIN : s * MAIN + 1]) for s in range(per)]
    for s in range(per):
        start = per * MAIN + s * TAIL
        parts.append(unmark(head[start : start + TAIL], head[s * MAIN : s * MAIN + 1]))
    head = jnp.concatenate(parts, axis=0).astype(piece.dtype)
    return jnp.concatenate([head, piece[:, LANES:]], axis=1), counts


def score_pieces(pieces, cols, weight_ref, per, slots, put):
    chunks, col_slides, _, width = cols.shape
    span = col_slides * CHUNK
    flat = cols[...].reshape(chunks * span, width)
    tile = lax.broadcasted_iota(jnp.int32, (1, slots), 1)
    lane = lax.broadcasted_iota(jnp.int32, (col_slides, span), 1)
    slide = lax.broadcasted_iota(jnp.int32, (col_slides, span), 0)
    clean = [clean_rows(piece[...], per) for piece in pieces]
    rows = jnp.concatenate([block for block, _ in clean], axis=0)
    score = lax.dot_general(rows, flat, NT, preferred_element_type=jnp.float32)
    parts = [score[:, k * span : (k + 1) * span] for k in range(chunks)]
    best = functools.reduce(jnp.maximum, parts)
    for t in range(len(pieces) * per):
        base, s = t // per * per * USED, t % per
        spots = (base + s * MAIN, MAIN), (base + per * MAIN + s * TAIL, TAIL)
        count = clean[t // per][1][s]
        mine = [best[start : start + size] for start, size in spots]
        mine = jnp.concatenate([*mine, jnp.zeros((slots - USED, span), jnp.float32)], axis=0).T
        mine = jnp.max(mine.reshape(col_slides, CHUNK, slots), axis=1)
        mine = jnp.where(tile.astype(jnp.float32) < count, mine, 0.0)
        back = []
        for k, part in enumerate(parts):
            highest = [jnp.max(part[start : start + size], axis=0, keepdims=True) for start, size in spots]
            back.append(functools.reduce(jnp.maximum, highest) * weight_ref[pl.ds(k, 1), :])
        back = jnp.where(lane // CHUNK == slide, functools.reduce(jnp.add, back), 0.0)
        mean = jnp.sum(mine * (0.5 / count), axis=1, keepdims=True) + jnp.sum(back, axis=1, keepdims=True)
        put(t, jnp.where(tile == slots - 1, mean, mine))


def first_kernel(count, labels, per, slots, *refs):
    pieces, blocks, (cols, weight_ref, out_ref) = refs[:count], refs[count:-3], refs[-3:]
    lay_columns(blocks, labels, per, cols, weight_ref)

    def put(t, best):
        out_ref[t] = best

    score_pieces(pieces, cols, weight_ref, per, slots, put)


def first_step(pieces, columns, labels, per, slots):
    count = len(pieces) * per
    chunks, width = slots // CHUNK, columns[0].shape[1]
    col_slides = sum(block.shape[0] for block in columns) // USED
    return pl.pallas_call(
        functools.partial(first_kernel, len(pieces), labels, per, slots),
        out_shape=(
            jax.ShapeDtypeStruct((chunks, col_slides, CHUNK, width), columns[0].dtype),
            jax.ShapeDtypeStruct((chunks, col_slides * CHUNK), jnp.float32),
            jax.ShapeDtypeStruct((count, col_slides, slots), jnp.float32),
        ),
        in_specs=[VMEM] * (len(pieces) + len(columns)),
        out_specs=(VMEM,) * 3,
        compiler_params=PARAMS,
        name="first_scores",
    )(*pieces, *columns)


def score_kernel(count, per, slots, *refs):
    pieces, (cols, weight_ref, out_ref) = refs[:count], refs[count:]

    def put(t, best):
        out_ref[t] = best

    score_pieces(pieces, cols, weight_ref, per, slots, put)


def score_step(pieces, cols, weight, per, slots):
    count = len(pieces) * per
    return pl.pallas_call(
        functools.partial(score_kernel, len(pieces), per, slots),
        out_shape=jax.ShapeDtypeStruct((count, cols.shape[1], slots), jnp.float32),
        in_specs=[VMEM] * (len(pieces) + 2),
        out_specs=VMEM,
        compiler_params=PARAMS,
        name="scores",
    )(*pieces, cols, weight)


def finish_kernel(size, groups, count, per, slots, *refs):
    pieces, (cols, weight_ref), refs = refs[:count], refs[count : count + 2], refs[count + 2 :]
    done, out_ref = refs[:-1], refs[-1]
    wide = out_ref.shape[2]
    block = lax.axis_index("dev") // groups
    first = sum(ref.shape[0] for ref in done)

    def keep(r, best):
        for g in range(groups):
            out_ref[g * (size // groups) + block, r] = best[g * wide : (g + 1) * wide]

    r = 0
    for ref in done:
        for n in range(ref.shape[0]):
            keep(r, ref[n])
            r += 1
    score_pieces(pieces, cols, weight_ref, per, slots, lambda t, best: keep(first + t, best))


def finish_step(pieces, cols, weight, done, size, groups, per, slots):
    count = len(pieces) * per + sum(part.shape[0] for part in done)
    wide = done[0].shape[1] // groups
    operands = [*pieces, cols, weight, *done]
    return pl.pallas_call(
        functools.partial(finish_kernel, size, groups, len(pieces), per, slots),
        out_shape=jax.ShapeDtypeStruct((size, count, wide, slots), jnp.float32),
        in_specs=[VMEM] * len(operands),
        out_specs=VMEM,
        compiler_params=PARAMS,
        name="finish",
    )(*operands)


def gather_kernel(size, groups, rows, parts, best_ref, chamfer_ref):
    slots = best_ref.shape[2]
    per = parts.shape[2] // 2
    first = lax.axis_index("dev") % (size // groups) * groups
    tile = lax.broadcasted_iota(jnp.int32, (1, slots), 1)
    lane = lax.broadcasted_iota(jnp.int32, (per, chamfer_ref.shape[1]), 1)
    means = [jnp.zeros((per, chamfer_ref.shape[1]), jnp.float32)] * groups
    for k in range(groups):
        for r, (mask, s) in enumerate(rows):
            a = ((first + k) ^ mask) * per + s
            part = parts[first + k, r]
            kept = jnp.where(tile < USED, part, 0.0)
            for pair in range(2):
                e = k ^ (2 * pair)
                best_ref[a, pl.ds(e * per, per), :] = kept[pair * per : (pair + 1) * per]
                mean = part[pair * per : (pair + 1) * per, slots - 1 :]
                means[e] = jnp.where(lane == a, mean, means[e])
    for e in range(groups):
        chamfer_ref[pl.ds(e * per, per), :] = means[e]


def gather_results(parts, rows, size, groups):
    _, count, wide, slots = parts.shape
    return pl.pallas_call(
        functools.partial(gather_kernel, size, groups, rows),
        out_shape=(
            jax.ShapeDtypeStruct((2 * count, groups * wide // 2, slots), jnp.float32),
            jax.ShapeDtypeStruct((groups * wide // 2, 2 * count), jnp.float32),
        ),
        in_specs=[VMEM],
        out_specs=(VMEM, VMEM),
        compiler_params=PARAMS,
        name="gather_results",
    )(parts)


def flip(value, axis, mask):
    return lax.ppermute(value, axis, [(i, i ^ mask) for i in range(lax.axis_size(axis))])


def relay_kernel(in_ref, out_ref):
    out_ref[...] = in_ref[...]


def relay(block):
    return pl.pallas_call(
        relay_kernel,
        out_shape=jax.ShapeDtypeStruct(block.shape, block.dtype),
        in_specs=[VMEM],
        out_specs=VMEM,
        compiler_params=PARAMS,
        name="relay",
    )(block)


def split_kernel(in_ref, *outs):
    start = 0
    for out_ref in outs:
        out_ref[...] = in_ref[pl.ds(start, out_ref.shape[0]), :]
        start += out_ref.shape[0]


def split_block(block, count):
    rows, width = block.shape
    ends = [-(-n * rows // (count * CHUNK)) * CHUNK for n in range(count + 1)]
    return pl.pallas_call(
        split_kernel,
        out_shape=[jax.ShapeDtypeStruct((end - start, width), block.dtype) for start, end in zip(ends, ends[1:])],
        in_specs=[VMEM],
        out_specs=[VMEM] * count,
        compiler_params=PARAMS,
        name="split_block",
    )(block)


def on_device(features, tile_counts, projection):
    size, groups = lax.axis_size("dev"), lax.axis_size("grp")
    slots = features.shape[1]
    whole = embed_tiles(features, tile_counts, projection)
    per = features.shape[0]
    across, beside = flip(whole, "dev", 1), flip(whole, "dev", 2)
    inner = [d for d in range(size) if (d >> 1 ^ d >> 2) & 1]
    outer = [d for d in range(size) if d not in inner]
    here = lax.axis_index("dev")
    within = (here >> 1 ^ here >> 2) & 1 == 1
    middle = lax.ppermute(whole, "dev", [(d, d ^ 6) for d in inner])
    beside, later = lax.optimization_barrier((beside, whole))
    edge = lax.ppermute(later, "dev", [(d, d ^ 6) for d in outer])
    labels, columns = [(0, 0, 0), (0, 1, 0)], [whole, beside]
    bit = groups // 2
    while bit > 1:
        columns += [flip(block, "grp", bit) for block in columns]
        labels += [(mask ^ bit, pair, 0) for mask, pair, _ in labels]
        bit //= 2
    cut = [2, 2, 1, 4]
    cut = [split_block(block, count) for block, count in zip(columns, cut + [2] * len(columns))]
    swapped = [flip(part, "grp", 1) for part in cut[0]]
    swapped, cut[-1] = lax.optimization_barrier((swapped, cut[-1]))
    middle, across, cut[-2] = lax.optimization_barrier((middle, across, cut[-2]))
    ends = [
        (part, (mask, pair, sum(other.shape[0] for other in parts[:n])))
        for parts, (mask, pair, _) in zip(cut, labels)
        for n, part in enumerate(parts)
    ]
    columns += swapped + [flip(part, "grp", 1) for part, _ in ends[len(swapped) :]]
    labels += [(mask ^ 1, pair, offset) for _, (mask, pair, offset) in ends]
    mirror = jnp.where(within, middle, edge)
    rows = [(whole, 0), (across, 1), (mirror, 6), (flip(mirror, "dev", 1), 7)]
    bit = 8
    while bit < size:
        rows += [(flip(block, "dev", bit), mask ^ bit) for block, mask in rows]
        bit *= 2
    blocks = [block for block, _ in rows]
    early, late = blocks[:-1], blocks[-1:]
    cols, weight, scored = first_step(early[:3], columns, labels, per, slots)
    done = [scored, *[score_step(early[i : i + 3], cols, weight, per, slots) for i in range(3, len(early), 3)]]
    results = finish_step(late, cols, weight, done, size, groups, per, slots)
    parts = lax.all_to_all(results, "dev", split_axis=0, concat_axis=0, tiled=True)
    names = tuple((mask, s) for _, mask in rows for s in range(per))
    best, chamfer = gather_results(parts, names, size, groups)
    return best, chamfer.T


def solution(mesh):
    return jax.shard_map(
        on_device,
        mesh=mesh,
        in_specs=(P(("grp", "dev"), None, None), P(("grp", "dev")), P()),
        out_specs=(P("grp", "dev", None), P("grp", "dev")),
        check_vma=False,
    )
```

```python
import functools

import jax
import jax.numpy as jnp
from jax import lax
from jax.experimental import pallas as pl
from jax.experimental.pallas import tpu as pltpu
from jax.sharding import PartitionSpec as P

USED = 120
CHUNK = 16
TAIL = 8
MAIN = USED - TAIL
MARK = 128.0
LANES = 128
VMEM_LIMIT = 40 * 1024 * 1024
NT = (((1,), (1,)), ((), ()))
VMEM = pl.BlockSpec(memory_space=pltpu.VMEM)
HBM = pl.BlockSpec(memory_space=pltpu.HBM)
PARAMS = pltpu.CompilerParams(vmem_limit_bytes=VMEM_LIMIT)


def embed_kernel(features_in, counts_in, projection_in, *refs):
    out_ref, features_ref, counts_ref, projection_ref, sems = refs
    copies = [
        pltpu.make_async_copy(projection_in, projection_ref, sems.at[0]),
        pltpu.make_async_copy(features_in, features_ref, sems.at[1]),
        pltpu.make_async_copy(counts_in, counts_ref, sems.at[2]),
    ]
    for copy in copies:
        copy.start()
    for copy in copies:
        copy.wait()
    slides, slots, _ = features_ref.shape
    tails = []
    for s in range(slides):
        raw = jnp.dot(features_ref[s], projection_ref[...], preferred_element_type=jnp.float32)
        scale = lax.rsqrt(jnp.sum(raw * raw, axis=1, keepdims=True) + 1e-06)
        unit = raw * scale
        slot = lax.broadcasted_iota(jnp.int32, unit.shape, 0)
        lane = lax.broadcasted_iota(jnp.int32, unit.shape, 1)
        count = counts_ref[s]
        unit = jnp.where(slot < count, unit, jnp.where(lane == 0, MARK + count.astype(jnp.float32), unit[:1]))
        out_ref[pl.ds(s * MAIN, MAIN), :] = unit[:MAIN].astype(out_ref.dtype)
        tails.append(unit[MAIN:USED])
    out_ref[pl.ds(slides * MAIN, slides * TAIL), :] = jnp.concatenate(tails, axis=0).astype(out_ref.dtype)


def embed_tiles(features, tile_counts, projection):
    slides = features.shape[0]
    width = projection.shape[1]
    return pl.pallas_call(
        embed_kernel,
        out_shape=jax.ShapeDtypeStruct((slides * USED, width), jnp.bfloat16),
        in_specs=[HBM] * 3,
        out_specs=VMEM,
        scratch_shapes=[
            pltpu.VMEM(features.shape, features.dtype),
            pltpu.SMEM(tile_counts.shape, tile_counts.dtype),
            pltpu.VMEM(projection.shape, projection.dtype),
            pltpu.SemaphoreType.DMA((3,)),
        ],
        compiler_params=PARAMS,
        name="embed",
    )(*[pltpu.with_memory_space_constraint(x, pltpu.HBM) for x in (features, tile_counts, projection)])


def slide_count(head, row):
    value = head[row : row + 1, :1]
    return jnp.where(value > 2.0, value - MARK, float(USED))


def unmark(head, top):
    column = lax.broadcasted_iota(jnp.int32, head.shape, 1)
    return jnp.where(jnp.logical_and(column == 0, head > 2.0), top, head)


def lay_columns(blocks, labels, per, cols, weight_ref):
    chunks, col_slides, _, _ = cols.shape
    span = col_slides * CHUNK
    lane = lax.broadcasted_iota(jnp.int32, (1, span), 1)
    counts = jnp.ones((1, span), jnp.float32)
    whole = {}
    for (mask, pair, offset), block in zip(labels, blocks):
        for start in range(0, block.shape[0], CHUNK):
            whole.setdefault((mask, pair), {})[offset + start] = block, start
    for place, parts in enumerate(whole.values()):
        first = place * per
        heads = {spot: ref[pl.ds(start, CHUNK), :LANES].astype(jnp.float32) for spot, (ref, start) in parts.items()}
        tops = [heads[s * MAIN][:1] for s in range(per)]
        for spot, (ref, start) in parts.items():
            if spot < per * MAIN:
                s, k = spot // MAIN, spot % MAIN // CHUNK
                cols[k, first + s, :, :LANES] = unmark(heads[spot], tops[s]).astype(cols.dtype)
                cols[k, first + s, :, LANES:] = ref[pl.ds(start, CHUNK), LANES:]
                continue
            tail = ref[pl.ds(start, CHUNK), :].astype(jnp.float32)
            for n in range(CHUNK // TAIL):
                s = (spot - per * MAIN) // TAIL + n
                count = slide_count(heads[spot], (n + 1) * TAIL - 1)
                counts = jnp.where(lane // CHUNK == first + s, count, counts)
                own = tail[n * TAIL : (n + 1) * TAIL]
                own = jnp.concatenate([unmark(own[:, :LANES], tops[s]), own[:, LANES:]], axis=1)
                cols[chunks - 1, first + s] = jnp.concatenate([own, own], axis=0).astype(cols.dtype)
    for k in range(chunks):
        tile = (k * CHUNK + lane % CHUNK).astype(jnp.float32)
        weight_ref[pl.ds(k, 1), :] = jnp.where(tile < counts, 0.5 / counts, 0.0)


def clean_rows(piece, per):
    head = piece[:, :LANES].astype(jnp.float32)
    counts = [slide_count(head, per * MAIN + (s + 1) * TAIL - 1) for s in range(per)]
    parts = [unmark(head[s * MAIN : (s + 1) * MAIN], head[s * MAIN : s * MAIN + 1]) for s in range(per)]
    for s in range(per):
        start = per * MAIN + s * TAIL
        parts.append(unmark(head[start : start + TAIL], head[s * MAIN : s * MAIN + 1]))
    head = jnp.concatenate(parts, axis=0).astype(piece.dtype)
    return jnp.concatenate([head, piece[:, LANES:]], axis=1), counts


def score_pieces(pieces, cols, weight_ref, per, slots, put):
    chunks, col_slides, _, width = cols.shape
    span = col_slides * CHUNK
    flat = cols[...].reshape(chunks * span, width)
    tile = lax.broadcasted_iota(jnp.int32, (1, slots), 1)
    lane = lax.broadcasted_iota(jnp.int32, (col_slides, span), 1)
    slide = lax.broadcasted_iota(jnp.int32, (col_slides, span), 0)
    clean = [clean_rows(piece[...], per) for piece in pieces]
    rows = jnp.concatenate([block for block, _ in clean], axis=0)
    score = lax.dot_general(rows, flat, NT, preferred_element_type=jnp.float32)
    parts = [score[:, k * span : (k + 1) * span] for k in range(chunks)]
    best = functools.reduce(jnp.maximum, parts)
    for t in range(len(pieces) * per):
        base, s = t // per * per * USED, t % per
        spots = (base + s * MAIN, MAIN), (base + per * MAIN + s * TAIL, TAIL)
        count = clean[t // per][1][s]
        mine = [best[start : start + size] for start, size in spots]
        mine = jnp.concatenate([*mine, jnp.zeros((slots - USED, span), jnp.float32)], axis=0).T
        mine = jnp.max(mine.reshape(col_slides, CHUNK, slots), axis=1)
        mine = jnp.where(tile.astype(jnp.float32) < count, mine, 0.0)
        back = []
        for k, part in enumerate(parts):
            highest = [jnp.max(part[start : start + size], axis=0, keepdims=True) for start, size in spots]
            back.append(functools.reduce(jnp.maximum, highest) * weight_ref[pl.ds(k, 1), :])
        back = jnp.where(lane // CHUNK == slide, functools.reduce(jnp.add, back), 0.0)
        mean = jnp.sum(mine * (0.5 / count), axis=1, keepdims=True) + jnp.sum(back, axis=1, keepdims=True)
        put(t, jnp.where(tile == slots - 1, mean, mine))


def first_kernel(count, labels, per, slots, *refs):
    pieces, blocks, (cols, weight_ref, out_ref) = refs[:count], refs[count:-3], refs[-3:]
    lay_columns(blocks, labels, per, cols, weight_ref)

    def put(t, best):
        out_ref[t] = best

    score_pieces(pieces, cols, weight_ref, per, slots, put)


def first_step(pieces, columns, labels, per, slots):
    count = len(pieces) * per
    chunks, width = slots // CHUNK, columns[0].shape[1]
    col_slides = sum(block.shape[0] for block in columns) // USED
    return pl.pallas_call(
        functools.partial(first_kernel, len(pieces), labels, per, slots),
        out_shape=(
            jax.ShapeDtypeStruct((chunks, col_slides, CHUNK, width), columns[0].dtype),
            jax.ShapeDtypeStruct((chunks, col_slides * CHUNK), jnp.float32),
            jax.ShapeDtypeStruct((count, col_slides, slots), jnp.float32),
        ),
        in_specs=[VMEM] * (len(pieces) + len(columns)),
        out_specs=(VMEM,) * 3,
        compiler_params=PARAMS,
        name="first_scores",
    )(*pieces, *columns)


def score_kernel(count, per, slots, *refs):
    pieces, (cols, weight_ref, out_ref) = refs[:count], refs[count:]

    def put(t, best):
        out_ref[t] = best

    score_pieces(pieces, cols, weight_ref, per, slots, put)


def score_step(pieces, cols, weight, per, slots):
    count = len(pieces) * per
    return pl.pallas_call(
        functools.partial(score_kernel, len(pieces), per, slots),
        out_shape=jax.ShapeDtypeStruct((count, cols.shape[1], slots), jnp.float32),
        in_specs=[VMEM] * (len(pieces) + 2),
        out_specs=VMEM,
        compiler_params=PARAMS,
        name="scores",
    )(*pieces, cols, weight)


def finish_kernel(size, groups, count, per, slots, labels, *refs):
    pieces, refs = refs[:count], refs[count:]
    sets, refs = [refs[2 * n : 2 * n + 2] for n in range(len(labels))], refs[2 * len(labels) :]
    done, out_ref = refs[:-1], refs[-1]
    block = lax.axis_index("dev") // groups
    mine = lax.axis_index("grp")

    def keep(n, r, best):
        for place, (mask, pair) in enumerate(labels[n]):
            part = best[place * per : (place + 1) * per]
            out_ref[(mine ^ mask) * (size // groups) + block, r, pl.ds(pair * per, per), :] = part

    for n in range(len(labels)):
        first = 0
        for ref in done[n :: len(labels)]:
            for r in range(ref.shape[0]):
                keep(n, first + r, ref[r])
            first += ref.shape[0]
        cols, weight_ref = sets[n]
        score_pieces(pieces, cols, weight_ref, per, slots, lambda t, best: keep(n, first + t, best))


def finish_step(pieces, sets, done, labels, size, groups, per, slots):
    count = len(pieces) * per + sum(part.shape[0] for part in done[:: len(labels)])
    operands = [*pieces, *[part for both in sets for part in both], *done]
    return pl.pallas_call(
        functools.partial(finish_kernel, size, groups, len(pieces), per, slots, labels),
        out_shape=jax.ShapeDtypeStruct((size, count, 2 * per, slots), jnp.float32),
        in_specs=[VMEM] * len(operands),
        out_specs=VMEM,
        compiler_params=PARAMS,
        name="finish",
    )(*operands)


def gather_kernel(size, groups, rows, parts, best_ref, chamfer_ref):
    slots = best_ref.shape[2]
    per = parts.shape[2] // 2
    first = lax.axis_index("dev") % (size // groups) * groups
    tile = lax.broadcasted_iota(jnp.int32, (1, slots), 1)
    lane = lax.broadcasted_iota(jnp.int32, (per, chamfer_ref.shape[1]), 1)
    means = [jnp.zeros((per, chamfer_ref.shape[1]), jnp.float32)] * groups
    for k in range(groups):
        for r, (mask, s) in enumerate(rows):
            a = ((first + k) ^ mask) * per + s
            part = parts[first + k, r]
            kept = jnp.where(tile < USED, part, 0.0)
            for pair in range(2):
                e = k ^ (2 * pair)
                best_ref[a, pl.ds(e * per, per), :] = kept[pair * per : (pair + 1) * per]
                mean = part[pair * per : (pair + 1) * per, slots - 1 :]
                means[e] = jnp.where(lane == a, mean, means[e])
    for e in range(groups):
        chamfer_ref[pl.ds(e * per, per), :] = means[e]


def gather_results(parts, rows, size, groups):
    _, count, wide, slots = parts.shape
    return pl.pallas_call(
        functools.partial(gather_kernel, size, groups, rows),
        out_shape=(
            jax.ShapeDtypeStruct((2 * count, groups * wide // 2, slots), jnp.float32),
            jax.ShapeDtypeStruct((groups * wide // 2, 2 * count), jnp.float32),
        ),
        in_specs=[VMEM],
        out_specs=(VMEM, VMEM),
        compiler_params=PARAMS,
        name="gather_results",
    )(parts)


def flip(value, axis, mask):
    return lax.ppermute(value, axis, [(i, i ^ mask) for i in range(lax.axis_size(axis))])


def relay_kernel(in_ref, out_ref):
    out_ref[...] = in_ref[...]


def relay(block):
    return pl.pallas_call(
        relay_kernel,
        out_shape=jax.ShapeDtypeStruct(block.shape, block.dtype),
        in_specs=[VMEM],
        out_specs=VMEM,
        compiler_params=PARAMS,
        name="relay",
    )(block)


def split_kernel(in_ref, *outs):
    start = 0
    for out_ref in outs:
        out_ref[...] = in_ref[pl.ds(start, out_ref.shape[0]), :]
        start += out_ref.shape[0]


def split_block(block, count):
    rows, width = block.shape
    ends = [-(-n * rows // (count * CHUNK)) * CHUNK for n in range(count + 1)]
    return pl.pallas_call(
        split_kernel,
        out_shape=[jax.ShapeDtypeStruct((end - start, width), block.dtype) for start, end in zip(ends, ends[1:])],
        in_specs=[VMEM],
        out_specs=[VMEM] * count,
        compiler_params=PARAMS,
        name="split_block",
    )(block)


def on_device(features, tile_counts, projection):
    size, groups = lax.axis_size("dev"), lax.axis_size("grp")
    slots = features.shape[1]
    whole = embed_tiles(features, tile_counts, projection)
    per = features.shape[0]
    mirror, across, beside = flip(whole, "dev", 6), flip(whole, "dev", 1), flip(whole, "dev", 2)
    labels, columns = [(0, 0, 0), (0, 1, 0)], [whole, beside]
    bit = groups // 2
    while bit > 1:
        columns += [flip(block, "grp", bit) for block in columns]
        labels += [(mask ^ bit, pair, 0) for mask, pair, _ in labels]
        bit //= 2
    cut = [2, 2, 2, 4]
    cut = [split_block(block, count) for block, count in zip(columns, cut + [2] * len(columns))]
    swapped = [[flip(part, "grp", 1) for part in cut[n]] for n in range(2)]
    rows = [(whole, 0), (across, 1), (mirror, 6), (flip(mirror, "dev", 1), 7)]
    bit = 8
    while bit < size:
        rows += [(flip(block, "dev", bit), mask ^ bit) for block, mask in rows]
        bit *= 2
    early, late = [block for block, _ in rows[:-1]], [block for block, _ in rows[-1:]]

    def column_set(which):
        blocks, names = [columns[n] for n in which], [labels[n] for n in which]
        for n in which:
            mask, pair, _ = labels[n]
            since = 0
            for part in swapped[n]:
                blocks.append(part)
                names.append((mask ^ 1, pair, since))
                since += part.shape[0]
        return blocks, tuple(names)

    near, near_names = column_set(range(2))
    *near_set, scored = first_step(early[:3], near, near_names, per, slots)
    scored, cut[-1] = lax.optimization_barrier((scored, cut[-1]))
    swapped += [[flip(part, "grp", 1) for part in parts] for parts in cut[2:]]
    far, far_names = column_set(range(2, len(columns)))
    *far_set, rest = first_step(early[:3], far, far_names, per, slots)
    sets, done = [near_set, far_set], [scored, rest]
    for i in range(3, len(early), 3):
        done += [score_step(early[i : i + 3], *both, per, slots) for both in sets]
    places = [tuple(dict.fromkeys((mask, pair) for mask, pair, _ in names)) for names in (near_names, far_names)]
    results = finish_step(late, sets, done, places, size, groups, per, slots)
    parts = lax.all_to_all(results, "dev", split_axis=0, concat_axis=0, tiled=True)
    names = tuple((mask, s) for _, mask in rows for s in range(per))
    best, chamfer = gather_results(parts, names, size, groups)
    return best, chamfer.T


def solution(mesh):
    return jax.shard_map(
        on_device,
        mesh=mesh,
        in_specs=(P(("grp", "dev"), None, None), P(("grp", "dev")), P()),
        out_specs=(P("grp", "dev", None), P("grp", "dev")),
        check_vma=False,
    )
```

```python
import functools

import jax
import jax.numpy as jnp
from jax import lax
from jax.experimental import pallas as pl
from jax.experimental.pallas import tpu as pltpu
from jax.sharding import PartitionSpec as P

USED = 120
CHUNK = 16
TAIL = 8
MAIN = USED - TAIL
MARK = 128.0
LANES = 128
VMEM_LIMIT = 40 * 1024 * 1024
NT = (((1,), (1,)), ((), ()))
VMEM = pl.BlockSpec(memory_space=pltpu.VMEM)
HBM = pl.BlockSpec(memory_space=pltpu.HBM)
PARAMS = pltpu.CompilerParams(vmem_limit_bytes=VMEM_LIMIT)


def embed_kernel(features_in, counts_in, projection_in, *refs):
    out_ref, features_ref, counts_ref, projection_ref, sems = refs
    copies = [
        pltpu.make_async_copy(projection_in, projection_ref, sems.at[0]),
        pltpu.make_async_copy(features_in, features_ref, sems.at[1]),
        pltpu.make_async_copy(counts_in, counts_ref, sems.at[2]),
    ]
    for copy in copies:
        copy.start()
    for copy in copies:
        copy.wait()
    slides, slots, _ = features_ref.shape
    tails = []
    for s in range(slides):
        raw = jnp.dot(features_ref[s], projection_ref[...], preferred_element_type=jnp.float32)
        scale = lax.rsqrt(jnp.sum(raw * raw, axis=1, keepdims=True) + 1e-06)
        unit = raw * scale
        slot = lax.broadcasted_iota(jnp.int32, unit.shape, 0)
        lane = lax.broadcasted_iota(jnp.int32, unit.shape, 1)
        count = counts_ref[s]
        unit = jnp.where(slot < count, unit, jnp.where(lane == 0, MARK + count.astype(jnp.float32), unit[:1]))
        out_ref[pl.ds(s * MAIN, MAIN), :] = unit[:MAIN].astype(out_ref.dtype)
        tails.append(unit[MAIN:USED])
    out_ref[pl.ds(slides * MAIN, slides * TAIL), :] = jnp.concatenate(tails, axis=0).astype(out_ref.dtype)


def embed_tiles(features, tile_counts, projection):
    slides = features.shape[0]
    width = projection.shape[1]
    return pl.pallas_call(
        embed_kernel,
        out_shape=jax.ShapeDtypeStruct((slides * USED, width), jnp.bfloat16),
        in_specs=[HBM] * 3,
        out_specs=VMEM,
        scratch_shapes=[
            pltpu.VMEM(features.shape, features.dtype),
            pltpu.SMEM(tile_counts.shape, tile_counts.dtype),
            pltpu.VMEM(projection.shape, projection.dtype),
            pltpu.SemaphoreType.DMA((3,)),
        ],
        compiler_params=PARAMS,
        name="embed",
    )(*[pltpu.with_memory_space_constraint(x, pltpu.HBM) for x in (features, tile_counts, projection)])


def slide_count(head, row):
    value = head[row : row + 1, :1]
    return jnp.where(value > 2.0, value - MARK, float(USED))


def unmark(head, top):
    column = lax.broadcasted_iota(jnp.int32, head.shape, 1)
    return jnp.where(jnp.logical_and(column == 0, head > 2.0), top, head)


def lay_columns(blocks, labels, per, cols, weight_ref):
    chunks, col_slides, _, _ = cols.shape
    span = col_slides * CHUNK
    lane = lax.broadcasted_iota(jnp.int32, (1, span), 1)
    counts = jnp.ones((1, span), jnp.float32)
    whole = {}
    for (mask, pair, offset), block in zip(labels, blocks):
        for start in range(0, block.shape[0], CHUNK):
            whole.setdefault((mask, pair), {})[offset + start] = block, start
    for place, parts in enumerate(whole.values()):
        first = place * per
        heads = {spot: ref[pl.ds(start, CHUNK), :LANES].astype(jnp.float32) for spot, (ref, start) in parts.items()}
        tops = [heads[s * MAIN][:1] for s in range(per)]
        for spot, (ref, start) in parts.items():
            if spot < per * MAIN:
                s, k = spot // MAIN, spot % MAIN // CHUNK
                cols[k, first + s, :, :LANES] = unmark(heads[spot], tops[s]).astype(cols.dtype)
                cols[k, first + s, :, LANES:] = ref[pl.ds(start, CHUNK), LANES:]
                continue
            tail = ref[pl.ds(start, CHUNK), :].astype(jnp.float32)
            for n in range(CHUNK // TAIL):
                s = (spot - per * MAIN) // TAIL + n
                count = slide_count(heads[spot], (n + 1) * TAIL - 1)
                counts = jnp.where(lane // CHUNK == first + s, count, counts)
                own = tail[n * TAIL : (n + 1) * TAIL]
                own = jnp.concatenate([unmark(own[:, :LANES], tops[s]), own[:, LANES:]], axis=1)
                cols[chunks - 1, first + s] = jnp.concatenate([own, own], axis=0).astype(cols.dtype)
    for k in range(chunks):
        tile = (k * CHUNK + lane % CHUNK).astype(jnp.float32)
        weight_ref[pl.ds(k, 1), :] = jnp.where(tile < counts, 0.5 / counts, 0.0)


def clean_rows(piece, per):
    head = piece[:, :LANES].astype(jnp.float32)
    counts = [slide_count(head, per * MAIN + (s + 1) * TAIL - 1) for s in range(per)]
    parts = [unmark(head[s * MAIN : (s + 1) * MAIN], head[s * MAIN : s * MAIN + 1]) for s in range(per)]
    for s in range(per):
        start = per * MAIN + s * TAIL
        parts.append(unmark(head[start : start + TAIL], head[s * MAIN : s * MAIN + 1]))
    head = jnp.concatenate(parts, axis=0).astype(piece.dtype)
    return jnp.concatenate([head, piece[:, LANES:]], axis=1), counts


def score_pieces(pieces, cols, weight_ref, per, slots, put):
    chunks, col_slides, _, width = cols.shape
    span = col_slides * CHUNK
    flat = cols[...].reshape(chunks * span, width)
    tile = lax.broadcasted_iota(jnp.int32, (1, slots), 1)
    lane = lax.broadcasted_iota(jnp.int32, (col_slides, span), 1)
    slide = lax.broadcasted_iota(jnp.int32, (col_slides, span), 0)
    clean = [clean_rows(piece[...], per) for piece in pieces]
    rows = jnp.concatenate([block for block, _ in clean], axis=0)
    score = lax.dot_general(rows, flat, NT, preferred_element_type=jnp.float32)
    parts = [score[:, k * span : (k + 1) * span] for k in range(chunks)]
    best = functools.reduce(jnp.maximum, parts)
    for t in range(len(pieces) * per):
        base, s = t // per * per * USED, t % per
        spots = (base + s * MAIN, MAIN), (base + per * MAIN + s * TAIL, TAIL)
        count = clean[t // per][1][s]
        mine = [best[start : start + size] for start, size in spots]
        mine = jnp.concatenate([*mine, jnp.zeros((slots - USED, span), jnp.float32)], axis=0).T
        mine = jnp.max(mine.reshape(col_slides, CHUNK, slots), axis=1)
        mine = jnp.where(tile.astype(jnp.float32) < count, mine, 0.0)
        back = []
        for k, part in enumerate(parts):
            highest = [jnp.max(part[start : start + size], axis=0, keepdims=True) for start, size in spots]
            back.append(functools.reduce(jnp.maximum, highest) * weight_ref[pl.ds(k, 1), :])
        back = jnp.where(lane // CHUNK == slide, functools.reduce(jnp.add, back), 0.0)
        mean = jnp.sum(mine * (0.5 / count), axis=1, keepdims=True) + jnp.sum(back, axis=1, keepdims=True)
        put(t, jnp.where(tile == slots - 1, mean, mine))


def first_kernel(count, labels, per, slots, *refs):
    pieces, blocks, (cols, weight_ref, out_ref) = refs[:count], refs[count:-3], refs[-3:]
    lay_columns(blocks, labels, per, cols, weight_ref)

    def put(t, best):
        out_ref[t] = best

    score_pieces(pieces, cols, weight_ref, per, slots, put)


def first_step(pieces, columns, labels, per, slots):
    count = len(pieces) * per
    chunks, width = slots // CHUNK, columns[0].shape[1]
    col_slides = sum(block.shape[0] for block in columns) // USED
    return pl.pallas_call(
        functools.partial(first_kernel, len(pieces), labels, per, slots),
        out_shape=(
            jax.ShapeDtypeStruct((chunks, col_slides, CHUNK, width), columns[0].dtype),
            jax.ShapeDtypeStruct((chunks, col_slides * CHUNK), jnp.float32),
            jax.ShapeDtypeStruct((count, col_slides, slots), jnp.float32),
        ),
        in_specs=[VMEM] * (len(pieces) + len(columns)),
        out_specs=(VMEM,) * 3,
        compiler_params=PARAMS,
        name="first_scores",
    )(*pieces, *columns)


def score_kernel(count, per, slots, *refs):
    pieces, (cols, weight_ref, out_ref) = refs[:count], refs[count:]

    def put(t, best):
        out_ref[t] = best

    score_pieces(pieces, cols, weight_ref, per, slots, put)


def score_step(pieces, cols, weight, per, slots):
    count = len(pieces) * per
    return pl.pallas_call(
        functools.partial(score_kernel, len(pieces), per, slots),
        out_shape=jax.ShapeDtypeStruct((count, cols.shape[1], slots), jnp.float32),
        in_specs=[VMEM] * (len(pieces) + 2),
        out_specs=VMEM,
        compiler_params=PARAMS,
        name="scores",
    )(*pieces, cols, weight)


def finish_kernel(size, groups, count, per, slots, labels, *refs):
    pieces, refs = refs[:count], refs[count:]
    sets, refs = [refs[2 * n : 2 * n + 2] for n in range(len(labels))], refs[2 * len(labels) :]
    done, out_ref = refs[:-1], refs[-1]
    block = lax.axis_index("dev") // groups
    mine = lax.axis_index("grp")

    def keep(n, r, best):
        for place, (mask, pair) in enumerate(labels[n]):
            part = best[place * per : (place + 1) * per]
            out_ref[(mine ^ mask) * (size // groups) + block, r, pl.ds(pair * per, per), :] = part

    for n in range(len(labels)):
        first = 0
        for ref in done[n :: len(labels)]:
            for r in range(ref.shape[0]):
                keep(n, first + r, ref[r])
            first += ref.shape[0]
        cols, weight_ref = sets[n]
        score_pieces(pieces, cols, weight_ref, per, slots, lambda t, best: keep(n, first + t, best))


def finish_step(pieces, sets, done, labels, size, groups, per, slots):
    count = len(pieces) * per + sum(part.shape[0] for part in done[:: len(labels)])
    operands = [*pieces, *[part for both in sets for part in both], *done]
    return pl.pallas_call(
        functools.partial(finish_kernel, size, groups, len(pieces), per, slots, labels),
        out_shape=jax.ShapeDtypeStruct((size, count, 2 * per, slots), jnp.float32),
        in_specs=[VMEM] * len(operands),
        out_specs=VMEM,
        compiler_params=PARAMS,
        name="finish",
    )(*operands)


def gather_kernel(size, groups, rows, parts, best_ref, chamfer_ref):
    slots = best_ref.shape[2]
    per = parts.shape[2] // 2
    first = lax.axis_index("dev") % (size // groups) * groups
    tile = lax.broadcasted_iota(jnp.int32, (1, slots), 1)
    lane = lax.broadcasted_iota(jnp.int32, (per, chamfer_ref.shape[1]), 1)
    means = [jnp.zeros((per, chamfer_ref.shape[1]), jnp.float32)] * groups
    for k in range(groups):
        for r, (mask, s) in enumerate(rows):
            a = ((first + k) ^ mask) * per + s
            part = parts[first + k, r]
            kept = jnp.where(tile < USED, part, 0.0)
            for pair in range(2):
                e = k ^ (2 * pair)
                best_ref[a, pl.ds(e * per, per), :] = kept[pair * per : (pair + 1) * per]
                mean = part[pair * per : (pair + 1) * per, slots - 1 :]
                means[e] = jnp.where(lane == a, mean, means[e])
    for e in range(groups):
        chamfer_ref[pl.ds(e * per, per), :] = means[e]


def gather_results(parts, rows, size, groups):
    _, count, wide, slots = parts.shape
    return pl.pallas_call(
        functools.partial(gather_kernel, size, groups, rows),
        out_shape=(
            jax.ShapeDtypeStruct((2 * count, groups * wide // 2, slots), jnp.float32),
            jax.ShapeDtypeStruct((groups * wide // 2, 2 * count), jnp.float32),
        ),
        in_specs=[VMEM],
        out_specs=(VMEM, VMEM),
        compiler_params=PARAMS,
        name="gather_results",
    )(parts)


def flip(value, axis, mask):
    return lax.ppermute(value, axis, [(i, i ^ mask) for i in range(lax.axis_size(axis))])


def relay_kernel(in_ref, out_ref):
    out_ref[...] = in_ref[...]


def relay(block):
    return pl.pallas_call(
        relay_kernel,
        out_shape=jax.ShapeDtypeStruct(block.shape, block.dtype),
        in_specs=[VMEM],
        out_specs=VMEM,
        compiler_params=PARAMS,
        name="relay",
    )(block)


def split_kernel(in_ref, *outs):
    start = 0
    for out_ref in outs:
        out_ref[...] = in_ref[pl.ds(start, out_ref.shape[0]), :]
        start += out_ref.shape[0]


def split_block(block, count):
    rows, width = block.shape
    ends = [-(-n * rows // (count * CHUNK)) * CHUNK for n in range(count + 1)]
    return pl.pallas_call(
        split_kernel,
        out_shape=[jax.ShapeDtypeStruct((end - start, width), block.dtype) for start, end in zip(ends, ends[1:])],
        in_specs=[VMEM],
        out_specs=[VMEM] * count,
        compiler_params=PARAMS,
        name="split_block",
    )(block)


def on_device(features, tile_counts, projection):
    size, groups = lax.axis_size("dev"), lax.axis_size("grp")
    slots = features.shape[1]
    whole = embed_tiles(features, tile_counts, projection)
    per = features.shape[0]
    opposite, across, beside = flip(whole, "dev", 4), flip(whole, "dev", 1), flip(whole, "dev", 2)
    labels, columns = [(0, 0, 0), (0, 1, 0)], [whole, beside]
    bit = groups // 2
    while bit > 1:
        columns += [flip(block, "grp", bit) for block in columns]
        labels += [(mask ^ bit, pair, 0) for mask, pair, _ in labels]
        bit //= 2
    cut = [2, 2, 2, 4]
    cut = [split_block(block, count) for block, count in zip(columns, cut + [2] * len(columns))]
    swapped = [[flip(part, "grp", 1) for part in cut[n]] for n in range(2)]
    rows = [(whole, 0), (across, 1), (opposite, 4), (flip(opposite, "dev", 1), 5)]
    bit = 8
    while bit < size:
        rows += [(flip(block, "dev", bit), mask ^ bit) for block, mask in rows]
        bit *= 2
    early, late = [block for block, _ in rows[:-1]], [block for block, _ in rows[-1:]]

    def column_set(which):
        blocks, names = [columns[n] for n in which], [labels[n] for n in which]
        for n in which:
            mask, pair, _ = labels[n]
            since = 0
            for part in swapped[n]:
                blocks.append(part)
                names.append((mask ^ 1, pair, since))
                since += part.shape[0]
        return blocks, tuple(names)

    near, near_names = column_set(range(2))
    *near_set, scored = first_step(early[:3], near, near_names, per, slots)
    scored, cut[-1] = lax.optimization_barrier((scored, cut[-1]))
    swapped += [[flip(part, "grp", 1) for part in parts] for parts in cut[2:]]
    far, far_names = column_set(range(2, len(columns)))
    *far_set, rest = first_step(early[:3], far, far_names, per, slots)
    sets, done = [near_set, far_set], [scored, rest]
    for i in range(3, len(early), 3):
        done += [score_step(early[i : i + 3], *both, per, slots) for both in sets]
    places = [tuple(dict.fromkeys((mask, pair) for mask, pair, _ in names)) for names in (near_names, far_names)]
    results = finish_step(late, sets, done, places, size, groups, per, slots)
    parts = lax.all_to_all(results, "dev", split_axis=0, concat_axis=0, tiled=True)
    names = tuple((mask, s) for _, mask in rows for s in range(per))
    best, chamfer = gather_results(parts, names, size, groups)
    return best, chamfer.T


def solution(mesh):
    return jax.shard_map(
        on_device,
        mesh=mesh,
        in_specs=(P(("grp", "dev"), None, None), P(("grp", "dev")), P()),
        out_specs=(P("grp", "dev", None), P("grp", "dev")),
        check_vma=False,
    )
```

```python
import functools

import jax
import jax.numpy as jnp
from jax import lax
from jax.experimental import pallas as pl
from jax.experimental.pallas import tpu as pltpu
from jax.sharding import PartitionSpec as P

USED = 120
CHUNK = 16
TAIL = 8
MAIN = USED - TAIL
MARK = 128.0
LANES = 128
VMEM_LIMIT = 40 * 1024 * 1024
NT = (((1,), (1,)), ((), ()))
VMEM = pl.BlockSpec(memory_space=pltpu.VMEM)
HBM = pl.BlockSpec(memory_space=pltpu.HBM)
PARAMS = pltpu.CompilerParams(vmem_limit_bytes=VMEM_LIMIT)


def part_sizes(rows, count):
    ends = [-(-n * rows // (count * CHUNK)) * CHUNK for n in range(count + 1)]
    return [end - start for start, end in zip(ends, ends[1:])]


def embed_kernel(features_in, counts_in, projection_in, *refs):
    (out_ref, *part_refs), (features_ref, counts_ref, projection_ref, sems) = refs[:-4], refs[-4:]
    copies = [
        pltpu.make_async_copy(projection_in, projection_ref, sems.at[0]),
        pltpu.make_async_copy(features_in, features_ref, sems.at[1]),
        pltpu.make_async_copy(counts_in, counts_ref, sems.at[2]),
    ]
    for copy in copies:
        copy.start()
    for copy in copies:
        copy.wait()
    slides, slots, depth = features_ref.shape
    tiles = features_ref[...].reshape(slides * slots, depth)
    every = jnp.dot(tiles, projection_ref[...], preferred_element_type=jnp.float32)
    tails = []
    for s in range(slides):
        raw = every[s * slots : (s + 1) * slots]
        scale = lax.rsqrt(jnp.sum(raw * raw, axis=1, keepdims=True) + 1e-06)
        unit = raw * scale
        slot = lax.broadcasted_iota(jnp.int32, unit.shape, 0)
        lane = lax.broadcasted_iota(jnp.int32, unit.shape, 1)
        count = counts_ref[s]
        unit = jnp.where(slot < count, unit, jnp.where(lane == 0, MARK + count.astype(jnp.float32), unit[:1]))
        out_ref[pl.ds(s * MAIN, MAIN), :] = unit[:MAIN].astype(out_ref.dtype)
        tails.append(unit[MAIN:USED])
    out_ref[pl.ds(slides * MAIN, slides * TAIL), :] = jnp.concatenate(tails, axis=0).astype(out_ref.dtype)
    start = 0
    for part_ref in part_refs:
        part_ref[...] = out_ref[pl.ds(start, part_ref.shape[0]), :]
        start += part_ref.shape[0]


def embed_tiles(features, tile_counts, projection):
    rows, width = features.shape[0] * USED, projection.shape[1]
    sizes = [rows, *part_sizes(rows, 2)]
    whole, *parts = pl.pallas_call(
        embed_kernel,
        out_shape=[jax.ShapeDtypeStruct((size, width), jnp.bfloat16) for size in sizes],
        in_specs=[HBM] * 3,
        out_specs=[VMEM] * len(sizes),
        scratch_shapes=[
            pltpu.VMEM(features.shape, features.dtype),
            pltpu.SMEM(tile_counts.shape, tile_counts.dtype),
            pltpu.VMEM(projection.shape, projection.dtype),
            pltpu.SemaphoreType.DMA((3,)),
        ],
        compiler_params=PARAMS,
        name="embed",
    )(*[pltpu.with_memory_space_constraint(x, pltpu.HBM) for x in (features, tile_counts, projection)])
    return whole, parts


def slide_count(head, row):
    value = head[row : row + 1, :1]
    return jnp.where(value > 2.0, value - MARK, float(USED))


def unmark(head, top):
    column = lax.broadcasted_iota(jnp.int32, head.shape, 1)
    return jnp.where(jnp.logical_and(column == 0, head > 2.0), top, head)


def lay_columns(blocks, labels, per, cols, weight_ref):
    chunks, col_slides, _, _ = cols.shape
    span = col_slides * CHUNK
    lane = lax.broadcasted_iota(jnp.int32, (1, span), 1)
    counts = jnp.ones((1, span), jnp.float32)
    whole = {}
    for (mask, pair, offset), block in zip(labels, blocks):
        for start in range(0, block.shape[0], CHUNK):
            whole.setdefault((mask, pair), {})[offset + start] = block, start
    for place, parts in enumerate(whole.values()):
        first = place * per
        heads = {spot: ref[pl.ds(start, CHUNK), :LANES].astype(jnp.float32) for spot, (ref, start) in parts.items()}
        tops = [heads[s * MAIN][:1] for s in range(per)]
        for spot, (ref, start) in parts.items():
            if spot < per * MAIN:
                s, k = spot // MAIN, spot % MAIN // CHUNK
                cols[k, first + s, :, :LANES] = unmark(heads[spot], tops[s]).astype(cols.dtype)
                cols[k, first + s, :, LANES:] = ref[pl.ds(start, CHUNK), LANES:]
                continue
            tail = ref[pl.ds(start, CHUNK), :].astype(jnp.float32)
            for n in range(CHUNK // TAIL):
                s = (spot - per * MAIN) // TAIL + n
                count = slide_count(heads[spot], (n + 1) * TAIL - 1)
                counts = jnp.where(lane // CHUNK == first + s, count, counts)
                own = tail[n * TAIL : (n + 1) * TAIL]
                own = jnp.concatenate([unmark(own[:, :LANES], tops[s]), own[:, LANES:]], axis=1)
                cols[chunks - 1, first + s] = jnp.concatenate([own, own], axis=0).astype(cols.dtype)
    for k in range(chunks):
        tile = (k * CHUNK + lane % CHUNK).astype(jnp.float32)
        weight_ref[pl.ds(k, 1), :] = jnp.where(tile < counts, 0.5 / counts, 0.0)


def clean_rows(piece, per):
    head = piece[:, :LANES].astype(jnp.float32)
    counts = [slide_count(head, per * MAIN + (s + 1) * TAIL - 1) for s in range(per)]
    parts = [unmark(head[s * MAIN : (s + 1) * MAIN], head[s * MAIN : s * MAIN + 1]) for s in range(per)]
    for s in range(per):
        start = per * MAIN + s * TAIL
        parts.append(unmark(head[start : start + TAIL], head[s * MAIN : s * MAIN + 1]))
    head = jnp.concatenate(parts, axis=0).astype(piece.dtype)
    return jnp.concatenate([head, piece[:, LANES:]], axis=1), counts


def score_pieces(pieces, cols, weight_ref, per, slots, put):
    chunks, col_slides, _, width = cols.shape
    span = col_slides * CHUNK
    flat = cols[...].reshape(chunks * span, width)
    tile = lax.broadcasted_iota(jnp.int32, (1, slots), 1)
    lane = lax.broadcasted_iota(jnp.int32, (col_slides, span), 1)
    slide = lax.broadcasted_iota(jnp.int32, (col_slides, span), 0)
    clean = [clean_rows(piece[...], per) for piece in pieces]
    rows = jnp.concatenate([block for block, _ in clean], axis=0)
    score = lax.dot_general(rows, flat, NT, preferred_element_type=jnp.float32)
    parts = [score[:, k * span : (k + 1) * span] for k in range(chunks)]
    best = functools.reduce(jnp.maximum, parts)
    for t in range(len(pieces) * per):
        base, s = t // per * per * USED, t % per
        spots = (base + s * MAIN, MAIN), (base + per * MAIN + s * TAIL, TAIL)
        count = clean[t // per][1][s]
        mine = [best[start : start + size] for start, size in spots]
        mine = jnp.concatenate([*mine, jnp.zeros((slots - USED, span), jnp.float32)], axis=0).T
        mine = jnp.max(mine.reshape(col_slides, CHUNK, slots), axis=1)
        mine = jnp.where(tile.astype(jnp.float32) < count, mine, 0.0)
        back = []
        for k, part in enumerate(parts):
            highest = [jnp.max(part[start : start + size], axis=0, keepdims=True) for start, size in spots]
            back.append(functools.reduce(jnp.maximum, highest) * weight_ref[pl.ds(k, 1), :])
        back = jnp.where(lane // CHUNK == slide, functools.reduce(jnp.add, back), 0.0)
        mean = jnp.sum(mine * (0.5 / count), axis=1, keepdims=True) + jnp.sum(back, axis=1, keepdims=True)
        put(t, jnp.where(tile == slots - 1, mean, mine))


def first_kernel(count, labels, per, slots, *refs):
    pieces, blocks, (cols, weight_ref, out_ref) = refs[:count], refs[count:-3], refs[-3:]
    lay_columns(blocks, labels, per, cols, weight_ref)

    def put(t, best):
        out_ref[t] = best

    score_pieces(pieces, cols, weight_ref, per, slots, put)


def first_step(pieces, columns, labels, per, slots):
    count = len(pieces) * per
    chunks, width = slots // CHUNK, columns[0].shape[1]
    col_slides = sum(block.shape[0] for block in columns) // USED
    return pl.pallas_call(
        functools.partial(first_kernel, len(pieces), labels, per, slots),
        out_shape=(
            jax.ShapeDtypeStruct((chunks, col_slides, CHUNK, width), columns[0].dtype),
            jax.ShapeDtypeStruct((chunks, col_slides * CHUNK), jnp.float32),
            jax.ShapeDtypeStruct((count, col_slides, slots), jnp.float32),
        ),
        in_specs=[VMEM] * (len(pieces) + len(columns)),
        out_specs=(VMEM,) * 3,
        compiler_params=PARAMS,
        name="first_scores",
    )(*pieces, *columns)


def score_kernel(count, per, slots, *refs):
    pieces, (cols, weight_ref, out_ref) = refs[:count], refs[count:]

    def put(t, best):
        out_ref[t] = best

    score_pieces(pieces, cols, weight_ref, per, slots, put)


def score_step(pieces, cols, weight, per, slots):
    count = len(pieces) * per
    return pl.pallas_call(
        functools.partial(score_kernel, len(pieces), per, slots),
        out_shape=jax.ShapeDtypeStruct((count, cols.shape[1], slots), jnp.float32),
        in_specs=[VMEM] * (len(pieces) + 2),
        out_specs=VMEM,
        compiler_params=PARAMS,
        name="scores",
    )(*pieces, cols, weight)


def finish_kernel(size, groups, count, per, slots, labels, *refs):
    pieces, refs = refs[:count], refs[count:]
    sets, refs = [refs[2 * n : 2 * n + 2] for n in range(len(labels))], refs[2 * len(labels) :]
    done, out_ref = refs[:-1], refs[-1]
    block = lax.axis_index("dev") // groups
    mine = lax.axis_index("grp")

    def keep(n, r, best):
        for place, (mask, pair) in enumerate(labels[n]):
            part = best[place * per : (place + 1) * per]
            out_ref[(mine ^ mask) * (size // groups) + block, r, pl.ds(pair * per, per), :] = part

    for n in range(len(labels)):
        first = 0
        for ref in done[n :: len(labels)]:
            for r in range(ref.shape[0]):
                keep(n, first + r, ref[r])
            first += ref.shape[0]
        cols, weight_ref = sets[n]
        score_pieces(pieces, cols, weight_ref, per, slots, lambda t, best: keep(n, first + t, best))


def finish_step(pieces, sets, done, labels, size, groups, per, slots):
    count = len(pieces) * per + sum(part.shape[0] for part in done[:: len(labels)])
    operands = [*pieces, *[part for both in sets for part in both], *done]
    return pl.pallas_call(
        functools.partial(finish_kernel, size, groups, len(pieces), per, slots, labels),
        out_shape=jax.ShapeDtypeStruct((size, count, 2 * per, slots), jnp.float32),
        in_specs=[VMEM] * len(operands),
        out_specs=VMEM,
        compiler_params=PARAMS,
        name="finish",
    )(*operands)


def gather_kernel(size, groups, rows, parts, best_ref, chamfer_ref):
    slots = best_ref.shape[2]
    per = parts.shape[2] // 2
    first = lax.axis_index("dev") % (size // groups) * groups
    tile = lax.broadcasted_iota(jnp.int32, (1, slots), 1)
    lane = lax.broadcasted_iota(jnp.int32, (per, chamfer_ref.shape[1]), 1)
    means = [jnp.zeros((per, chamfer_ref.shape[1]), jnp.float32)] * groups
    for k in range(groups):
        for r, (mask, s) in enumerate(rows):
            a = ((first + k) ^ mask) * per + s
            part = parts[first + k, r]
            kept = jnp.where(tile < USED, part, 0.0)
            for pair in range(2):
                e = k ^ (2 * pair)
                best_ref[a, pl.ds(e * per, per), :] = kept[pair * per : (pair + 1) * per]
                mean = part[pair * per : (pair + 1) * per, slots - 1 :]
                means[e] = jnp.where(lane == a, mean, means[e])
    for e in range(groups):
        chamfer_ref[pl.ds(e * per, per), :] = means[e]


def gather_results(parts, rows, size, groups):
    _, count, wide, slots = parts.shape
    return pl.pallas_call(
        functools.partial(gather_kernel, size, groups, rows),
        out_shape=(
            jax.ShapeDtypeStruct((2 * count, groups * wide // 2, slots), jnp.float32),
            jax.ShapeDtypeStruct((groups * wide // 2, 2 * count), jnp.float32),
        ),
        in_specs=[VMEM],
        out_specs=(VMEM, VMEM),
        compiler_params=PARAMS,
        name="gather_results",
    )(parts)


def flip(value, axis, mask):
    return lax.ppermute(value, axis, [(i, i ^ mask) for i in range(lax.axis_size(axis))])


def relay_kernel(in_ref, out_ref):
    out_ref[...] = in_ref[...]


def relay(block):
    return pl.pallas_call(
        relay_kernel,
        out_shape=jax.ShapeDtypeStruct(block.shape, block.dtype),
        in_specs=[VMEM],
        out_specs=VMEM,
        compiler_params=PARAMS,
        name="relay",
    )(block)


def split_kernel(in_ref, *outs):
    start = 0
    for out_ref in outs:
        out_ref[...] = in_ref[pl.ds(start, out_ref.shape[0]), :]
        start += out_ref.shape[0]


def split_block(block, count):
    rows, width = block.shape
    return pl.pallas_call(
        split_kernel,
        out_shape=[jax.ShapeDtypeStruct((size, width), block.dtype) for size in part_sizes(rows, count)],
        in_specs=[VMEM],
        out_specs=[VMEM] * count,
        compiler_params=PARAMS,
        name="split_block",
    )(block)


def on_device(features, tile_counts, projection):
    size, groups = lax.axis_size("dev"), lax.axis_size("grp")
    slots = features.shape[1]
    whole, halves = embed_tiles(features, tile_counts, projection)
    per = features.shape[0]
    opposite, across, beside = flip(whole, "dev", 4), flip(whole, "dev", 1), flip(whole, "dev", 2)
    labels, columns = [(0, 0, 0), (0, 1, 0)], [whole, beside]
    bit = groups // 2
    while bit > 1:
        columns += [flip(block, "grp", bit) for block in columns]
        labels += [(mask ^ bit, pair, 0) for mask, pair, _ in labels]
        bit //= 2
    cut = [2, 2, 2, 3]
    cut = [halves] + [split_block(block, count) for block, count in zip(columns[1:], cut[1:] + [2] * len(columns))]
    swapped = [[flip(part, "grp", 1) for part in cut[n]] for n in range(2)]
    rows = [(whole, 0), (across, 1), (opposite, 4), (flip(opposite, "dev", 1), 5)]
    bit = 8
    while bit < size:
        rows += [(flip(block, "dev", bit), mask ^ bit) for block, mask in rows]
        bit *= 2
    early, late = [block for block, _ in rows[:-1]], [block for block, _ in rows[-1:]]

    def column_set(which):
        blocks, names = [columns[n] for n in which], [labels[n] for n in which]
        for n in which:
            mask, pair, _ = labels[n]
            since = 0
            for part in swapped[n]:
                blocks.append(part)
                names.append((mask ^ 1, pair, since))
                since += part.shape[0]
        return blocks, tuple(names)

    near, near_names = column_set(range(2))
    *near_set, scored = first_step(early[:3], near, near_names, per, slots)
    scored, cut[-1] = lax.optimization_barrier((scored, cut[-1]))
    swapped += [[flip(part, "grp", 1) for part in parts] for parts in cut[2:]]
    far, far_names = column_set(range(2, len(columns)))
    *far_set, rest = first_step(early[:3], far, far_names, per, slots)
    sets, done = [near_set, far_set], [scored, rest]
    for i in range(3, len(early), 3):
        done += [score_step(early[i : i + 3], *both, per, slots) for both in sets]
    places = [tuple(dict.fromkeys((mask, pair) for mask, pair, _ in names)) for names in (near_names, far_names)]
    results = finish_step(late, sets, done, places, size, groups, per, slots)
    parts = lax.all_to_all(results, "dev", split_axis=0, concat_axis=0, tiled=True)
    names = tuple((mask, s) for _, mask in rows for s in range(per))
    best, chamfer = gather_results(parts, names, size, groups)
    return best, chamfer.T


def solution(mesh):
    return jax.shard_map(
        on_device,
        mesh=mesh,
        in_specs=(P(("grp", "dev"), None, None), P(("grp", "dev")), P()),
        out_specs=(P("grp", "dev", None), P("grp", "dev")),
        check_vma=False,
    )
```

```python
import functools

import jax
import jax.numpy as jnp
from jax import lax
from jax.experimental import pallas as pl
from jax.experimental.pallas import tpu as pltpu
from jax.sharding import PartitionSpec as P

USED = 120
CHUNK = 16
TAIL = 8
MAIN = USED - TAIL
MARK = 128.0
LANES = 128
VMEM_LIMIT = 40 * 1024 * 1024
NT = (((1,), (1,)), ((), ()))
VMEM = pl.BlockSpec(memory_space=pltpu.VMEM)
HBM = pl.BlockSpec(memory_space=pltpu.HBM)
PARAMS = pltpu.CompilerParams(vmem_limit_bytes=VMEM_LIMIT)


def part_sizes(rows, count):
    ends = [-(-n * rows // (count * CHUNK)) * CHUNK for n in range(count + 1)]
    return [end - start for start, end in zip(ends, ends[1:])]


def embed_kernel(features_in, counts_in, projection_in, *refs):
    (out_ref, *part_refs), (features_ref, counts_ref, projection_ref, sems) = refs[:-4], refs[-4:]
    copies = [
        pltpu.make_async_copy(projection_in, projection_ref, sems.at[0]),
        pltpu.make_async_copy(features_in, features_ref, sems.at[1]),
        pltpu.make_async_copy(counts_in, counts_ref, sems.at[2]),
    ]
    for copy in copies:
        copy.start()
    for copy in copies:
        copy.wait()
    slides, slots, depth = features_ref.shape
    tiles = features_ref[...].reshape(slides * slots, depth)
    every = jnp.dot(tiles, projection_ref[...], preferred_element_type=jnp.float32)
    tails = []
    for s in range(slides):
        raw = every[s * slots : (s + 1) * slots]
        scale = lax.rsqrt(jnp.sum(raw * raw, axis=1, keepdims=True) + 1e-06)
        unit = raw * scale
        slot = lax.broadcasted_iota(jnp.int32, unit.shape, 0)
        lane = lax.broadcasted_iota(jnp.int32, unit.shape, 1)
        count = counts_ref[s]
        unit = jnp.where(slot < count, unit, jnp.where(lane == 0, MARK + count.astype(jnp.float32), unit[:1]))
        out_ref[pl.ds(s * MAIN, MAIN), :] = unit[:MAIN].astype(out_ref.dtype)
        tails.append(unit[MAIN:USED])
    out_ref[pl.ds(slides * MAIN, slides * TAIL), :] = jnp.concatenate(tails, axis=0).astype(out_ref.dtype)
    start = 0
    for part_ref in part_refs:
        part_ref[...] = out_ref[pl.ds(start, part_ref.shape[0]), :]
        start += part_ref.shape[0]


def embed_tiles(features, tile_counts, projection):
    rows, width = features.shape[0] * USED, projection.shape[1]
    sizes = [rows, *part_sizes(rows, 2)]
    whole, *parts = pl.pallas_call(
        embed_kernel,
        out_shape=[jax.ShapeDtypeStruct((size, width), jnp.bfloat16) for size in sizes],
        in_specs=[HBM] * 3,
        out_specs=[VMEM] * len(sizes),
        scratch_shapes=[
            pltpu.VMEM(features.shape, features.dtype),
            pltpu.SMEM(tile_counts.shape, tile_counts.dtype),
            pltpu.VMEM(projection.shape, projection.dtype),
            pltpu.SemaphoreType.DMA((3,)),
        ],
        compiler_params=PARAMS,
        name="embed",
    )(*[pltpu.with_memory_space_constraint(x, pltpu.HBM) for x in (features, tile_counts, projection)])
    return whole, parts


def slide_count(head, row):
    value = head[row : row + 1, :1]
    return jnp.where(value > 2.0, value - MARK, float(USED))


def unmark(head, top):
    column = lax.broadcasted_iota(jnp.int32, head.shape, 1)
    return jnp.where(jnp.logical_and(column == 0, head > 2.0), top, head)


def lay_columns(blocks, labels, per, cols, weight_ref):
    chunks, col_slides, _, _ = cols.shape
    span = col_slides * CHUNK
    lane = lax.broadcasted_iota(jnp.int32, (1, span), 1)
    counts = jnp.ones((1, span), jnp.float32)
    whole = {}
    for (mask, pair, offset), block in zip(labels, blocks):
        for start in range(0, block.shape[0], CHUNK):
            whole.setdefault((mask, pair), {})[offset + start] = block, start
    for place, parts in enumerate(whole.values()):
        first = place * per
        heads = {spot: ref[pl.ds(start, CHUNK), :LANES].astype(jnp.float32) for spot, (ref, start) in parts.items()}
        tops = [heads[s * MAIN][:1] for s in range(per)]
        for spot, (ref, start) in parts.items():
            if spot < per * MAIN:
                s, k = spot // MAIN, spot % MAIN // CHUNK
                cols[k, first + s, :, :LANES] = unmark(heads[spot], tops[s]).astype(cols.dtype)
                cols[k, first + s, :, LANES:] = ref[pl.ds(start, CHUNK), LANES:]
                continue
            tail = ref[pl.ds(start, CHUNK), :].astype(jnp.float32)
            for n in range(CHUNK // TAIL):
                s = (spot - per * MAIN) // TAIL + n
                count = slide_count(heads[spot], (n + 1) * TAIL - 1)
                counts = jnp.where(lane // CHUNK == first + s, count, counts)
                own = tail[n * TAIL : (n + 1) * TAIL]
                own = jnp.concatenate([unmark(own[:, :LANES], tops[s]), own[:, LANES:]], axis=1)
                cols[chunks - 1, first + s] = jnp.concatenate([own, own], axis=0).astype(cols.dtype)
    for k in range(chunks):
        tile = (k * CHUNK + lane % CHUNK).astype(jnp.float32)
        weight_ref[pl.ds(k, 1), :] = jnp.where(tile < counts, 0.5 / counts, 0.0)


def clean_rows(piece, per):
    head = piece[:, :LANES].astype(jnp.float32)
    counts = [slide_count(head, per * MAIN + (s + 1) * TAIL - 1) for s in range(per)]
    parts = [unmark(head[s * MAIN : (s + 1) * MAIN], head[s * MAIN : s * MAIN + 1]) for s in range(per)]
    for s in range(per):
        start = per * MAIN + s * TAIL
        parts.append(unmark(head[start : start + TAIL], head[s * MAIN : s * MAIN + 1]))
    head = jnp.concatenate(parts, axis=0).astype(piece.dtype)
    return jnp.concatenate([head, piece[:, LANES:]], axis=1), counts


def score_pieces(pieces, cols, weight_ref, per, slots, put):
    chunks, col_slides, _, width = cols.shape
    span = col_slides * CHUNK
    flat = cols[...].reshape(chunks * span, width)
    tile = lax.broadcasted_iota(jnp.int32, (1, slots), 1)
    lane = lax.broadcasted_iota(jnp.int32, (col_slides, span), 1)
    slide = lax.broadcasted_iota(jnp.int32, (col_slides, span), 0)
    clean = [clean_rows(piece[...], per) for piece in pieces]
    rows = jnp.concatenate([block for block, _ in clean], axis=0)
    score = lax.dot_general(rows, flat, NT, preferred_element_type=jnp.float32)
    parts = [score[:, k * span : (k + 1) * span] for k in range(chunks)]
    best = functools.reduce(jnp.maximum, parts)
    for t in range(len(pieces) * per):
        base, s = t // per * per * USED, t % per
        spots = (base + s * MAIN, MAIN), (base + per * MAIN + s * TAIL, TAIL)
        count = clean[t // per][1][s]
        mine = [best[start : start + size] for start, size in spots]
        mine = jnp.concatenate([*mine, jnp.zeros((slots - USED, span), jnp.float32)], axis=0).T
        mine = jnp.max(mine.reshape(col_slides, CHUNK, slots), axis=1)
        mine = jnp.where(tile.astype(jnp.float32) < count, mine, 0.0)
        back = []
        for k, part in enumerate(parts):
            highest = [jnp.max(part[start : start + size], axis=0, keepdims=True) for start, size in spots]
            back.append(functools.reduce(jnp.maximum, highest) * weight_ref[pl.ds(k, 1), :])
        back = jnp.where(lane // CHUNK == slide, functools.reduce(jnp.add, back), 0.0)
        mean = jnp.sum(mine * (0.5 / count), axis=1, keepdims=True) + jnp.sum(back, axis=1, keepdims=True)
        put(t, jnp.where(tile == slots - 1, mean, mine))


def first_kernel(count, labels, per, slots, *refs):
    pieces, blocks, (cols, weight_ref, out_ref) = refs[:count], refs[count:-3], refs[-3:]
    lay_columns(blocks, labels, per, cols, weight_ref)

    def put(t, best):
        out_ref[t] = best

    score_pieces(pieces, cols, weight_ref, per, slots, put)


def first_step(pieces, columns, labels, per, slots):
    count = len(pieces) * per
    chunks, width = slots // CHUNK, columns[0].shape[1]
    col_slides = sum(block.shape[0] for block in columns) // USED
    return pl.pallas_call(
        functools.partial(first_kernel, len(pieces), labels, per, slots),
        out_shape=(
            jax.ShapeDtypeStruct((chunks, col_slides, CHUNK, width), columns[0].dtype),
            jax.ShapeDtypeStruct((chunks, col_slides * CHUNK), jnp.float32),
            jax.ShapeDtypeStruct((count, col_slides, slots), jnp.float32),
        ),
        in_specs=[VMEM] * (len(pieces) + len(columns)),
        out_specs=(VMEM,) * 3,
        compiler_params=PARAMS,
        name="first_scores",
    )(*pieces, *columns)


def score_kernel(count, per, slots, *refs):
    pieces, (cols, weight_ref, out_ref) = refs[:count], refs[count:]

    def put(t, best):
        out_ref[t] = best

    score_pieces(pieces, cols, weight_ref, per, slots, put)


def score_step(pieces, cols, weight, per, slots):
    count = len(pieces) * per
    return pl.pallas_call(
        functools.partial(score_kernel, len(pieces), per, slots),
        out_shape=jax.ShapeDtypeStruct((count, cols.shape[1], slots), jnp.float32),
        in_specs=[VMEM] * (len(pieces) + 2),
        out_specs=VMEM,
        compiler_params=PARAMS,
        name="scores",
    )(*pieces, cols, weight)


def finish_kernel(size, groups, count, per, slots, labels, *refs):
    pieces, refs = refs[:count], refs[count:]
    sets, refs = [refs[2 * n : 2 * n + 2] for n in range(len(labels))], refs[2 * len(labels) :]
    done, out_ref = refs[:-1], refs[-1]
    block = lax.axis_index("dev") // groups
    mine = lax.axis_index("grp")

    def keep(n, r, best):
        for place, (mask, pair) in enumerate(labels[n]):
            part = best[place * per : (place + 1) * per]
            out_ref[(mine ^ mask) * (size // groups) + block, r, pl.ds(pair * per, per), :] = part

    for n in range(len(labels)):
        first = 0
        for ref in done[n :: len(labels)]:
            for r in range(ref.shape[0]):
                keep(n, first + r, ref[r])
            first += ref.shape[0]
        cols, weight_ref = sets[n]
        score_pieces(pieces, cols, weight_ref, per, slots, lambda t, best: keep(n, first + t, best))


def finish_step(pieces, sets, done, labels, size, groups, per, slots):
    count = len(pieces) * per + sum(part.shape[0] for part in done[:: len(labels)])
    operands = [*pieces, *[part for both in sets for part in both], *done]
    return pl.pallas_call(
        functools.partial(finish_kernel, size, groups, len(pieces), per, slots, labels),
        out_shape=jax.ShapeDtypeStruct((size, count, 2 * per, slots), jnp.float32),
        in_specs=[VMEM] * len(operands),
        out_specs=VMEM,
        compiler_params=PARAMS,
        name="finish",
    )(*operands)


def gather_kernel(size, groups, rows, parts, best_ref, chamfer_ref):
    slots = best_ref.shape[2]
    per = parts.shape[2] // 2
    first = lax.axis_index("dev") % (size // groups) * groups
    tile = lax.broadcasted_iota(jnp.int32, (1, slots), 1)
    lane = lax.broadcasted_iota(jnp.int32, (per, chamfer_ref.shape[1]), 1)
    means = [jnp.zeros((per, chamfer_ref.shape[1]), jnp.float32)] * groups
    for k in range(groups):
        for r, (mask, s) in enumerate(rows):
            a = ((first + k) ^ mask) * per + s
            part = parts[first + k, r]
            kept = jnp.where(tile < USED, part, 0.0)
            for pair in range(2):
                e = k ^ (2 * pair)
                best_ref[a, pl.ds(e * per, per), :] = kept[pair * per : (pair + 1) * per]
                mean = part[pair * per : (pair + 1) * per, slots - 1 :]
                means[e] = jnp.where(lane == a, mean, means[e])
    for e in range(groups):
        chamfer_ref[pl.ds(e * per, per), :] = means[e]


def gather_results(parts, rows, size, groups):
    _, count, wide, slots = parts.shape
    return pl.pallas_call(
        functools.partial(gather_kernel, size, groups, rows),
        out_shape=(
            jax.ShapeDtypeStruct((2 * count, groups * wide // 2, slots), jnp.float32),
            jax.ShapeDtypeStruct((groups * wide // 2, 2 * count), jnp.float32),
        ),
        in_specs=[VMEM],
        out_specs=(VMEM, VMEM),
        compiler_params=PARAMS,
        name="gather_results",
    )(parts)


def flip(value, axis, mask):
    return lax.ppermute(value, axis, [(i, i ^ mask) for i in range(lax.axis_size(axis))])


def relay_kernel(in_ref, out_ref):
    out_ref[...] = in_ref[...]


def relay(block):
    return pl.pallas_call(
        relay_kernel,
        out_shape=jax.ShapeDtypeStruct(block.shape, block.dtype),
        in_specs=[VMEM],
        out_specs=VMEM,
        compiler_params=PARAMS,
        name="relay",
    )(block)


def split_kernel(in_ref, *outs):
    start = 0
    for out_ref in outs:
        out_ref[...] = in_ref[pl.ds(start, out_ref.shape[0]), :]
        start += out_ref.shape[0]


def split_block(block, count):
    rows, width = block.shape
    return pl.pallas_call(
        split_kernel,
        out_shape=[jax.ShapeDtypeStruct((size, width), block.dtype) for size in part_sizes(rows, count)],
        in_specs=[VMEM],
        out_specs=[VMEM] * count,
        compiler_params=PARAMS,
        name="split_block",
    )(block)


def on_device(features, tile_counts, projection):
    size, groups = lax.axis_size("dev"), lax.axis_size("grp")
    slots = features.shape[1]
    whole, halves = embed_tiles(features, tile_counts, projection)
    per = features.shape[0]
    opposite, across, beside = flip(whole, "dev", 6), flip(whole, "dev", 1), flip(whole, "dev", 2)
    labels, columns = [(0, 0, 0), (0, 1, 0)], [whole, beside]
    bit = groups // 2
    while bit > 1:
        columns += [flip(block, "grp", bit) for block in columns]
        labels += [(mask ^ bit, pair, 0) for mask, pair, _ in labels]
        bit //= 2
    cut = [2, 2, 2, 3]
    cut = [halves] + [split_block(block, count) for block, count in zip(columns[1:], cut[1:] + [2] * len(columns))]
    swapped = [[flip(part, "grp", 1) for part in cut[n]] for n in range(2)]
    rows = [(whole, 0), (across, 1), (opposite, 6), (flip(opposite, "dev", 1), 7)]
    bit = 8
    while bit < size:
        rows += [(flip(block, "dev", bit), mask ^ bit) for block, mask in rows]
        bit *= 2
    early, late = [block for block, _ in rows[:-1]], [block for block, _ in rows[-1:]]

    def column_set(which):
        blocks, names = [columns[n] for n in which], [labels[n] for n in which]
        for n in which:
            mask, pair, _ = labels[n]
            since = 0
            for part in swapped[n]:
                blocks.append(part)
                names.append((mask ^ 1, pair, since))
                since += part.shape[0]
        return blocks, tuple(names)

    near, near_names = column_set(range(2))
    *near_set, scored = first_step(early[:3], near, near_names, per, slots)
    scored, cut[-1] = lax.optimization_barrier((scored, cut[-1]))
    swapped += [[flip(part, "grp", 1) for part in parts] for parts in cut[2:]]
    far, far_names = column_set(range(2, len(columns)))
    *far_set, rest = first_step(early[:3], far, far_names, per, slots)
    sets, done = [near_set, far_set], [scored, rest]
    for i in range(3, len(early), 3):
        done += [score_step(early[i : i + 3], *both, per, slots) for both in sets]
    places = [tuple(dict.fromkeys((mask, pair) for mask, pair, _ in names)) for names in (near_names, far_names)]
    results = finish_step(late, sets, done, places, size, groups, per, slots)
    parts = lax.all_to_all(results, "dev", split_axis=0, concat_axis=0, tiled=True)
    names = tuple((mask, s) for _, mask in rows for s in range(per))
    best, chamfer = gather_results(parts, names, size, groups)
    return best, chamfer.T


def solution(mesh):
    return jax.shard_map(
        on_device,
        mesh=mesh,
        in_specs=(P(("grp", "dev"), None, None), P(("grp", "dev")), P()),
        out_specs=(P("grp", "dev", None), P("grp", "dev")),
        check_vma=False,
    )
```

```python
import functools

import jax
import jax.numpy as jnp
from jax import lax
from jax.experimental import pallas as pl
from jax.experimental.pallas import tpu as pltpu
from jax.sharding import PartitionSpec as P

USED = 120
CHUNK = 16
TAIL = 8
MAIN = USED - TAIL
MARK = 128.0
LANES = 128
PIECE = 256
VMEM_LIMIT = 40 * 1024 * 1024
NT = (((1,), (1,)), ((), ()))
VMEM = pl.BlockSpec(memory_space=pltpu.VMEM)
HBM = pl.BlockSpec(memory_space=pltpu.HBM)
PARAMS = pltpu.CompilerParams(vmem_limit_bytes=VMEM_LIMIT)


def part_sizes(rows, count):
    ends = [-(-n * rows // (count * CHUNK)) * CHUNK for n in range(count + 1)]
    return [end - start for start, end in zip(ends, ends[1:])]


def embed_kernel(features_in, counts_in, projection_in, *refs):
    (out_ref, *part_refs), (features_ref, counts_ref, projection_ref, sems) = refs[:-4], refs[-4:]
    slides, slots, depth = features_ref.shape
    pieces = [pl.ds(start, PIECE) for start in range(0, depth, PIECE)]
    first = [
        pltpu.make_async_copy(features_in, features_ref, sems.at[0]),
        pltpu.make_async_copy(counts_in, counts_ref, sems.at[1]),
    ]
    loads = [
        pltpu.make_async_copy(projection_in.at[piece], projection_ref.at[piece], sems.at[2 + n])
        for n, piece in enumerate(pieces)
    ]
    for copy in first + loads:
        copy.start()
    for copy in first:
        copy.wait()
    tiles = features_ref[...].reshape(slides * slots, depth)
    every = jnp.zeros((slides * slots, projection_ref.shape[1]), jnp.float32)
    for n, piece in enumerate(pieces):
        loads[n].wait()
        part = tiles[:, n * PIECE : (n + 1) * PIECE]
        every = every + jnp.dot(part, projection_ref[piece, :], preferred_element_type=jnp.float32)
    tails = []
    for s in range(slides):
        raw = every[s * slots : (s + 1) * slots]
        scale = lax.rsqrt(jnp.sum(raw * raw, axis=1, keepdims=True) + 1e-06)
        unit = raw * scale
        slot = lax.broadcasted_iota(jnp.int32, unit.shape, 0)
        lane = lax.broadcasted_iota(jnp.int32, unit.shape, 1)
        count = counts_ref[s]
        unit = jnp.where(slot < count, unit, jnp.where(lane == 0, MARK + count.astype(jnp.float32), unit[:1]))
        out_ref[pl.ds(s * MAIN, MAIN), :] = unit[:MAIN].astype(out_ref.dtype)
        tails.append(unit[MAIN:USED])
    out_ref[pl.ds(slides * MAIN, slides * TAIL), :] = jnp.concatenate(tails, axis=0).astype(out_ref.dtype)
    start = 0
    for part_ref in part_refs:
        part_ref[...] = out_ref[pl.ds(start, part_ref.shape[0]), :]
        start += part_ref.shape[0]


def embed_tiles(features, tile_counts, projection):
    rows, width = features.shape[0] * USED, projection.shape[1]
    sizes = [rows, *part_sizes(rows, 2)]
    whole, *parts = pl.pallas_call(
        embed_kernel,
        out_shape=[jax.ShapeDtypeStruct((size, width), jnp.bfloat16) for size in sizes],
        in_specs=[HBM] * 3,
        out_specs=[VMEM] * len(sizes),
        scratch_shapes=[
            pltpu.VMEM(features.shape, features.dtype),
            pltpu.SMEM(tile_counts.shape, tile_counts.dtype),
            pltpu.VMEM(projection.shape, projection.dtype),
            pltpu.SemaphoreType.DMA((2 + projection.shape[0] // PIECE,)),
        ],
        compiler_params=PARAMS,
        name="embed",
    )(*[pltpu.with_memory_space_constraint(x, pltpu.HBM) for x in (features, tile_counts, projection)])
    return whole, parts


def slide_count(head, row):
    value = head[row : row + 1, :1]
    return jnp.where(value > 2.0, value - MARK, float(USED))


def unmark(head, top):
    column = lax.broadcasted_iota(jnp.int32, head.shape, 1)
    return jnp.where(jnp.logical_and(column == 0, head > 2.0), top, head)


def lay_columns(blocks, labels, per, cols, weight_ref):
    chunks, col_slides, _, _ = cols.shape
    span = col_slides * CHUNK
    lane = lax.broadcasted_iota(jnp.int32, (1, span), 1)
    counts = jnp.ones((1, span), jnp.float32)
    whole = {}
    for (mask, pair, offset), block in zip(labels, blocks):
        for start in range(0, block.shape[0], CHUNK):
            whole.setdefault((mask, pair), {})[offset + start] = block, start
    for place, parts in enumerate(whole.values()):
        first = place * per
        heads = {spot: ref[pl.ds(start, CHUNK), :LANES].astype(jnp.float32) for spot, (ref, start) in parts.items()}
        tops = [heads[s * MAIN][:1] for s in range(per)]
        for spot, (ref, start) in parts.items():
            if spot < per * MAIN:
                s, k = spot // MAIN, spot % MAIN // CHUNK
                cols[k, first + s, :, :LANES] = unmark(heads[spot], tops[s]).astype(cols.dtype)
                cols[k, first + s, :, LANES:] = ref[pl.ds(start, CHUNK), LANES:]
                continue
            tail = ref[pl.ds(start, CHUNK), :].astype(jnp.float32)
            for n in range(CHUNK // TAIL):
                s = (spot - per * MAIN) // TAIL + n
                count = slide_count(heads[spot], (n + 1) * TAIL - 1)
                counts = jnp.where(lane // CHUNK == first + s, count, counts)
                own = tail[n * TAIL : (n + 1) * TAIL]
                own = jnp.concatenate([unmark(own[:, :LANES], tops[s]), own[:, LANES:]], axis=1)
                cols[chunks - 1, first + s] = jnp.concatenate([own, own], axis=0).astype(cols.dtype)
    for k in range(chunks):
        tile = (k * CHUNK + lane % CHUNK).astype(jnp.float32)
        weight_ref[pl.ds(k, 1), :] = jnp.where(tile < counts, 0.5 / counts, 0.0)


def clean_rows(piece, per):
    head = piece[:, :LANES].astype(jnp.float32)
    counts = [slide_count(head, per * MAIN + (s + 1) * TAIL - 1) for s in range(per)]
    parts = [unmark(head[s * MAIN : (s + 1) * MAIN], head[s * MAIN : s * MAIN + 1]) for s in range(per)]
    for s in range(per):
        start = per * MAIN + s * TAIL
        parts.append(unmark(head[start : start + TAIL], head[s * MAIN : s * MAIN + 1]))
    head = jnp.concatenate(parts, axis=0).astype(piece.dtype)
    return jnp.concatenate([head, piece[:, LANES:]], axis=1), counts


def score_pieces(pieces, cols, weight_ref, per, slots, put):
    chunks, col_slides, _, width = cols.shape
    span = col_slides * CHUNK
    flat = cols[...].reshape(chunks * span, width)
    tile = lax.broadcasted_iota(jnp.int32, (1, slots), 1)
    lane = lax.broadcasted_iota(jnp.int32, (col_slides, span), 1)
    slide = lax.broadcasted_iota(jnp.int32, (col_slides, span), 0)
    clean = [clean_rows(piece[...], per) for piece in pieces]
    rows = jnp.concatenate([block for block, _ in clean], axis=0)
    score = lax.dot_general(rows, flat, NT, preferred_element_type=jnp.float32)
    parts = [score[:, k * span : (k + 1) * span] for k in range(chunks)]
    best = functools.reduce(jnp.maximum, parts)
    for t in range(len(pieces) * per):
        base, s = t // per * per * USED, t % per
        spots = (base + s * MAIN, MAIN), (base + per * MAIN + s * TAIL, TAIL)
        count = clean[t // per][1][s]
        mine = [best[start : start + size] for start, size in spots]
        mine = jnp.concatenate([*mine, jnp.zeros((slots - USED, span), jnp.float32)], axis=0).T
        mine = jnp.max(mine.reshape(col_slides, CHUNK, slots), axis=1)
        mine = jnp.where(tile.astype(jnp.float32) < count, mine, 0.0)
        back = []
        for k, part in enumerate(parts):
            highest = [jnp.max(part[start : start + size], axis=0, keepdims=True) for start, size in spots]
            back.append(functools.reduce(jnp.maximum, highest) * weight_ref[pl.ds(k, 1), :])
        back = jnp.where(lane // CHUNK == slide, functools.reduce(jnp.add, back), 0.0)
        mean = jnp.sum(mine * (0.5 / count), axis=1, keepdims=True) + jnp.sum(back, axis=1, keepdims=True)
        put(t, jnp.where(tile == slots - 1, mean, mine))


def first_kernel(count, labels, per, slots, *refs):
    pieces, blocks, (cols, weight_ref, out_ref) = refs[:count], refs[count:-3], refs[-3:]
    lay_columns(blocks, labels, per, cols, weight_ref)

    def put(t, best):
        out_ref[t] = best

    score_pieces(pieces, cols, weight_ref, per, slots, put)


def first_step(pieces, columns, labels, per, slots):
    count = len(pieces) * per
    chunks, width = slots // CHUNK, columns[0].shape[1]
    col_slides = sum(block.shape[0] for block in columns) // USED
    return pl.pallas_call(
        functools.partial(first_kernel, len(pieces), labels, per, slots),
        out_shape=(
            jax.ShapeDtypeStruct((chunks, col_slides, CHUNK, width), columns[0].dtype),
            jax.ShapeDtypeStruct((chunks, col_slides * CHUNK), jnp.float32),
            jax.ShapeDtypeStruct((count, col_slides, slots), jnp.float32),
        ),
        in_specs=[VMEM] * (len(pieces) + len(columns)),
        out_specs=(VMEM,) * 3,
        compiler_params=PARAMS,
        name="first_scores",
    )(*pieces, *columns)


def score_kernel(count, per, slots, *refs):
    pieces, (cols, weight_ref, out_ref) = refs[:count], refs[count:]

    def put(t, best):
        out_ref[t] = best

    score_pieces(pieces, cols, weight_ref, per, slots, put)


def score_step(pieces, cols, weight, per, slots):
    count = len(pieces) * per
    return pl.pallas_call(
        functools.partial(score_kernel, len(pieces), per, slots),
        out_shape=jax.ShapeDtypeStruct((count, cols.shape[1], slots), jnp.float32),
        in_specs=[VMEM] * (len(pieces) + 2),
        out_specs=VMEM,
        compiler_params=PARAMS,
        name="scores",
    )(*pieces, cols, weight)


def finish_kernel(size, groups, count, per, slots, labels, *refs):
    pieces, refs = refs[:count], refs[count:]
    sets, refs = [refs[2 * n : 2 * n + 2] for n in range(len(labels))], refs[2 * len(labels) :]
    done, out_ref = refs[:-1], refs[-1]
    block = lax.axis_index("dev") // groups
    mine = lax.axis_index("grp")

    def keep(n, r, best):
        for place, (mask, pair) in enumerate(labels[n]):
            part = best[place * per : (place + 1) * per]
            out_ref[(mine ^ mask) * (size // groups) + block, r, pl.ds(pair * per, per), :] = part

    for n in range(len(labels)):
        first = 0
        for ref in done[n :: len(labels)]:
            for r in range(ref.shape[0]):
                keep(n, first + r, ref[r])
            first += ref.shape[0]
        cols, weight_ref = sets[n]
        score_pieces(pieces, cols, weight_ref, per, slots, lambda t, best: keep(n, first + t, best))


def finish_step(pieces, sets, done, labels, size, groups, per, slots):
    count = len(pieces) * per + sum(part.shape[0] for part in done[:: len(labels)])
    operands = [*pieces, *[part for both in sets for part in both], *done]
    return pl.pallas_call(
        functools.partial(finish_kernel, size, groups, len(pieces), per, slots, labels),
        out_shape=jax.ShapeDtypeStruct((size, count, 2 * per, slots), jnp.float32),
        in_specs=[VMEM] * len(operands),
        out_specs=VMEM,
        compiler_params=PARAMS,
        name="finish",
    )(*operands)


def gather_kernel(size, groups, rows, parts, best_ref, chamfer_ref):
    slots = best_ref.shape[2]
    per = parts.shape[2] // 2
    first = lax.axis_index("dev") % (size // groups) * groups
    tile = lax.broadcasted_iota(jnp.int32, (1, slots), 1)
    lane = lax.broadcasted_iota(jnp.int32, (per, chamfer_ref.shape[1]), 1)
    means = [jnp.zeros((per, chamfer_ref.shape[1]), jnp.float32)] * groups
    for k in range(groups):
        for r, (mask, s) in enumerate(rows):
            a = ((first + k) ^ mask) * per + s
            part = parts[first + k, r]
            kept = jnp.where(tile < USED, part, 0.0)
            for pair in range(2):
                e = k ^ (2 * pair)
                best_ref[a, pl.ds(e * per, per), :] = kept[pair * per : (pair + 1) * per]
                mean = part[pair * per : (pair + 1) * per, slots - 1 :]
                means[e] = jnp.where(lane == a, mean, means[e])
    for e in range(groups):
        chamfer_ref[pl.ds(e * per, per), :] = means[e]


def gather_results(parts, rows, size, groups):
    _, count, wide, slots = parts.shape
    return pl.pallas_call(
        functools.partial(gather_kernel, size, groups, rows),
        out_shape=(
            jax.ShapeDtypeStruct((2 * count, groups * wide // 2, slots), jnp.float32),
            jax.ShapeDtypeStruct((groups * wide // 2, 2 * count), jnp.float32),
        ),
        in_specs=[VMEM],
        out_specs=(VMEM, VMEM),
        compiler_params=PARAMS,
        name="gather_results",
    )(parts)


def flip(value, axis, mask):
    return lax.ppermute(value, axis, [(i, i ^ mask) for i in range(lax.axis_size(axis))])


def relay_kernel(in_ref, out_ref):
    out_ref[...] = in_ref[...]


def relay(block):
    return pl.pallas_call(
        relay_kernel,
        out_shape=jax.ShapeDtypeStruct(block.shape, block.dtype),
        in_specs=[VMEM],
        out_specs=VMEM,
        compiler_params=PARAMS,
        name="relay",
    )(block)


def split_kernel(in_ref, *outs):
    start = 0
    for out_ref in outs:
        out_ref[...] = in_ref[pl.ds(start, out_ref.shape[0]), :]
        start += out_ref.shape[0]


def split_block(block, count):
    rows, width = block.shape
    return pl.pallas_call(
        split_kernel,
        out_shape=[jax.ShapeDtypeStruct((size, width), block.dtype) for size in part_sizes(rows, count)],
        in_specs=[VMEM],
        out_specs=[VMEM] * count,
        compiler_params=PARAMS,
        name="split_block",
    )(block)


def on_device(features, tile_counts, projection):
    size, groups = lax.axis_size("dev"), lax.axis_size("grp")
    slots = features.shape[1]
    whole, halves = embed_tiles(features, tile_counts, projection)
    per = features.shape[0]
    opposite, across, beside = flip(whole, "dev", 4), flip(whole, "dev", 1), flip(whole, "dev", 2)
    labels, columns = [(0, 0, 0), (0, 1, 0)], [whole, beside]
    bit = groups // 2
    while bit > 1:
        columns += [flip(block, "grp", bit) for block in columns]
        labels += [(mask ^ bit, pair, 0) for mask, pair, _ in labels]
        bit //= 2
    cut = [2, 2, 2, 3]
    cut = [halves] + [split_block(block, count) for block, count in zip(columns[1:], cut[1:] + [2] * len(columns))]
    swapped = [[flip(part, "grp", 1) for part in cut[n]] for n in range(2)]
    rows = [(whole, 0), (across, 1), (opposite, 4), (flip(opposite, "dev", 1), 5)]
    bit = 8
    while bit < size:
        rows += [(flip(block, "dev", bit), mask ^ bit) for block, mask in rows]
        bit *= 2
    early, late = [block for block, _ in rows[:-1]], [block for block, _ in rows[-1:]]

    def column_set(which):
        blocks, names = [columns[n] for n in which], [labels[n] for n in which]
        for n in which:
            mask, pair, _ = labels[n]
            since = 0
            for part in swapped[n]:
                blocks.append(part)
                names.append((mask ^ 1, pair, since))
                since += part.shape[0]
        return blocks, tuple(names)

    near, near_names = column_set(range(2))
    *near_set, scored = first_step(early[:3], near, near_names, per, slots)
    scored, cut[-1] = lax.optimization_barrier((scored, cut[-1]))
    swapped += [[flip(part, "grp", 1) for part in parts] for parts in cut[2:]]
    far, far_names = column_set(range(2, len(columns)))
    *far_set, rest = first_step(early[:3], far, far_names, per, slots)
    sets, done = [near_set, far_set], [scored, rest]
    for i in range(3, len(early), 3):
        done += [score_step(early[i : i + 3], *both, per, slots) for both in sets]
    places = [tuple(dict.fromkeys((mask, pair) for mask, pair, _ in names)) for names in (near_names, far_names)]
    results = finish_step(late, sets, done, places, size, groups, per, slots)
    parts = lax.all_to_all(results, "dev", split_axis=0, concat_axis=0, tiled=True)
    names = tuple((mask, s) for _, mask in rows for s in range(per))
    best, chamfer = gather_results(parts, names, size, groups)
    return best, chamfer.T


def solution(mesh):
    return jax.shard_map(
        on_device,
        mesh=mesh,
        in_specs=(P(("grp", "dev"), None, None), P(("grp", "dev")), P()),
        out_specs=(P("grp", "dev", None), P("grp", "dev")),
        check_vma=False,
    )
```

```python
import functools

import jax
import jax.numpy as jnp
from jax import lax
from jax.experimental import pallas as pl
from jax.experimental.pallas import tpu as pltpu
from jax.sharding import PartitionSpec as P

USED = 120
CHUNK = 16
TAIL = 8
MAIN = USED - TAIL
MARK = 128.0
LANES = 128
VMEM_LIMIT = 40 * 1024 * 1024
NT = (((1,), (1,)), ((), ()))
VMEM = pl.BlockSpec(memory_space=pltpu.VMEM)
HBM = pl.BlockSpec(memory_space=pltpu.HBM)
PARAMS = pltpu.CompilerParams(vmem_limit_bytes=VMEM_LIMIT)


def part_sizes(rows, count):
    ends = [-(-n * rows // (count * CHUNK)) * CHUNK for n in range(count + 1)]
    return [end - start for start, end in zip(ends, ends[1:])]


def embed_kernel(features_in, counts_in, projection_in, *refs):
    (out_ref, *part_refs), (features_ref, counts_ref, projection_ref, sems) = refs[:-4], refs[-4:]
    copies = [
        pltpu.make_async_copy(projection_in, projection_ref, sems.at[0]),
        pltpu.make_async_copy(features_in, features_ref, sems.at[1]),
        pltpu.make_async_copy(counts_in, counts_ref, sems.at[2]),
    ]
    for copy in copies:
        copy.start()
    for copy in copies:
        copy.wait()
    slides, slots, depth = features_ref.shape
    tiles = features_ref[...].reshape(slides * slots, depth)
    every = jnp.dot(tiles, projection_ref[...], preferred_element_type=jnp.float32)
    tails = []
    for s in range(slides):
        raw = every[s * slots : (s + 1) * slots]
        scale = lax.rsqrt(jnp.sum(raw * raw, axis=1, keepdims=True) + 1e-06)
        unit = raw * scale
        slot = lax.broadcasted_iota(jnp.int32, unit.shape, 0)
        lane = lax.broadcasted_iota(jnp.int32, unit.shape, 1)
        count = counts_ref[s]
        unit = jnp.where(slot < count, unit, jnp.where(lane == 0, MARK + count.astype(jnp.float32), unit[:1]))
        out_ref[pl.ds(s * MAIN, MAIN), :] = unit[:MAIN].astype(out_ref.dtype)
        tails.append(unit[MAIN:USED])
    out_ref[pl.ds(slides * MAIN, slides * TAIL), :] = jnp.concatenate(tails, axis=0).astype(out_ref.dtype)
    start = 0
    for part_ref in part_refs:
        part_ref[...] = out_ref[pl.ds(start, part_ref.shape[0]), :]
        start += part_ref.shape[0]


def embed_tiles(features, tile_counts, projection):
    rows, width = features.shape[0] * USED, projection.shape[1]
    sizes = [rows, *part_sizes(rows, 2)]
    whole, *parts = pl.pallas_call(
        embed_kernel,
        out_shape=[jax.ShapeDtypeStruct((size, width), jnp.bfloat16) for size in sizes],
        in_specs=[HBM] * 3,
        out_specs=[VMEM] * len(sizes),
        scratch_shapes=[
            pltpu.VMEM(features.shape, features.dtype),
            pltpu.SMEM(tile_counts.shape, tile_counts.dtype),
            pltpu.VMEM(projection.shape, projection.dtype),
            pltpu.SemaphoreType.DMA((3,)),
        ],
        compiler_params=PARAMS,
        name="embed",
    )(*[pltpu.with_memory_space_constraint(x, pltpu.HBM) for x in (features, tile_counts, projection)])
    return whole, parts


def slide_count(head, row):
    value = head[row : row + 1, :1]
    return jnp.where(value > 2.0, value - MARK, float(USED))


def unmark(head, top):
    column = lax.broadcasted_iota(jnp.int32, head.shape, 1)
    return jnp.where(jnp.logical_and(column == 0, head > 2.0), top, head)


def lay_columns(blocks, labels, per, cols, weight_ref):
    chunks, col_slides, _, _ = cols.shape
    span = col_slides * CHUNK
    lane = lax.broadcasted_iota(jnp.int32, (1, span), 1)
    counts = jnp.ones((1, span), jnp.float32)
    whole = {}
    for (mask, pair, offset), block in zip(labels, blocks):
        for start in range(0, block.shape[0], CHUNK):
            whole.setdefault((mask, pair), {})[offset + start] = block, start
    for place, parts in enumerate(whole.values()):
        first = place * per
        heads = {spot: ref[pl.ds(start, CHUNK), :LANES].astype(jnp.float32) for spot, (ref, start) in parts.items()}
        tops = [heads[s * MAIN][:1] for s in range(per)]
        for spot, (ref, start) in parts.items():
            if spot < per * MAIN:
                s, k = spot // MAIN, spot % MAIN // CHUNK
                cols[k, first + s, :, :LANES] = unmark(heads[spot], tops[s]).astype(cols.dtype)
                cols[k, first + s, :, LANES:] = ref[pl.ds(start, CHUNK), LANES:]
                continue
            tail = ref[pl.ds(start, CHUNK), :].astype(jnp.float32)
            for n in range(CHUNK // TAIL):
                s = (spot - per * MAIN) // TAIL + n
                count = slide_count(heads[spot], (n + 1) * TAIL - 1)
                counts = jnp.where(lane // CHUNK == first + s, count, counts)
                own = tail[n * TAIL : (n + 1) * TAIL]
                own = jnp.concatenate([unmark(own[:, :LANES], tops[s]), own[:, LANES:]], axis=1)
                cols[chunks - 1, first + s] = jnp.concatenate([own, own], axis=0).astype(cols.dtype)
    for k in range(chunks):
        tile = (k * CHUNK + lane % CHUNK).astype(jnp.float32)
        weight_ref[pl.ds(k, 1), :] = jnp.where(tile < counts, 0.5 / counts, 0.0)


def clean_rows(piece, per):
    head = piece[:, :LANES].astype(jnp.float32)
    counts = [slide_count(head, per * MAIN + (s + 1) * TAIL - 1) for s in range(per)]
    parts = [unmark(head[s * MAIN : (s + 1) * MAIN], head[s * MAIN : s * MAIN + 1]) for s in range(per)]
    for s in range(per):
        start = per * MAIN + s * TAIL
        parts.append(unmark(head[start : start + TAIL], head[s * MAIN : s * MAIN + 1]))
    head = jnp.concatenate(parts, axis=0).astype(piece.dtype)
    return jnp.concatenate([head, piece[:, LANES:]], axis=1), counts


def score_pieces(pieces, cols, weight_ref, per, slots, put):
    chunks, col_slides, _, width = cols.shape
    span = col_slides * CHUNK
    flat = cols[...].reshape(chunks * span, width)
    tile = lax.broadcasted_iota(jnp.int32, (1, slots), 1)
    lane = lax.broadcasted_iota(jnp.int32, (col_slides, span), 1)
    slide = lax.broadcasted_iota(jnp.int32, (col_slides, span), 0)
    clean = [clean_rows(piece[...], per) for piece in pieces]
    rows = jnp.concatenate([block for block, _ in clean], axis=0)
    score = lax.dot_general(rows, flat, NT, preferred_element_type=jnp.float32)
    parts = [score[:, k * span : (k + 1) * span] for k in range(chunks)]
    best = functools.reduce(jnp.maximum, parts)
    for t in range(len(pieces) * per):
        base, s = t // per * per * USED, t % per
        spots = (base + s * MAIN, MAIN), (base + per * MAIN + s * TAIL, TAIL)
        count = clean[t // per][1][s]
        mine = [best[start : start + size] for start, size in spots]
        mine = jnp.concatenate([*mine, jnp.zeros((slots - USED, span), jnp.float32)], axis=0).T
        mine = jnp.max(mine.reshape(col_slides, CHUNK, slots), axis=1)
        mine = jnp.where(tile.astype(jnp.float32) < count, mine, 0.0)
        back = []
        for k, part in enumerate(parts):
            highest = [jnp.max(part[start : start + size], axis=0, keepdims=True) for start, size in spots]
            back.append(functools.reduce(jnp.maximum, highest) * weight_ref[pl.ds(k, 1), :])
        back = jnp.where(lane // CHUNK == slide, functools.reduce(jnp.add, back), 0.0)
        mean = jnp.sum(mine * (0.5 / count), axis=1, keepdims=True) + jnp.sum(back, axis=1, keepdims=True)
        put(t, jnp.where(tile == slots - 1, mean, mine))


def first_kernel(count, labels, per, slots, *refs):
    pieces, blocks, (cols, weight_ref, out_ref) = refs[:count], refs[count:-3], refs[-3:]
    lay_columns(blocks, labels, per, cols, weight_ref)

    def put(t, best):
        out_ref[t] = best

    score_pieces(pieces, cols, weight_ref, per, slots, put)


def first_step(pieces, columns, labels, per, slots):
    count = len(pieces) * per
    chunks, width = slots // CHUNK, columns[0].shape[1]
    col_slides = sum(block.shape[0] for block in columns) // USED
    return pl.pallas_call(
        functools.partial(first_kernel, len(pieces), labels, per, slots),
        out_shape=(
            jax.ShapeDtypeStruct((chunks, col_slides, CHUNK, width), columns[0].dtype),
            jax.ShapeDtypeStruct((chunks, col_slides * CHUNK), jnp.float32),
            jax.ShapeDtypeStruct((count, col_slides, slots), jnp.float32),
        ),
        in_specs=[VMEM] * (len(pieces) + len(columns)),
        out_specs=(VMEM,) * 3,
        compiler_params=PARAMS,
        name="first_scores",
    )(*pieces, *columns)


def score_kernel(count, per, slots, *refs):
    pieces, (cols, weight_ref, out_ref) = refs[:count], refs[count:]

    def put(t, best):
        out_ref[t] = best

    score_pieces(pieces, cols, weight_ref, per, slots, put)


def score_step(pieces, cols, weight, per, slots):
    count = len(pieces) * per
    return pl.pallas_call(
        functools.partial(score_kernel, len(pieces), per, slots),
        out_shape=jax.ShapeDtypeStruct((count, cols.shape[1], slots), jnp.float32),
        in_specs=[VMEM] * (len(pieces) + 2),
        out_specs=VMEM,
        compiler_params=PARAMS,
        name="scores",
    )(*pieces, cols, weight)


def finish_kernel(size, groups, count, per, slots, labels, *refs):
    pieces, refs = refs[:count], refs[count:]
    sets, refs = [refs[2 * n : 2 * n + 2] for n in range(len(labels))], refs[2 * len(labels) :]
    done, out_ref = refs[:-1], refs[-1]
    block = lax.axis_index("dev") // groups
    mine = lax.axis_index("grp")

    def keep(n, r, best):
        for place, (mask, pair) in enumerate(labels[n]):
            part = best[place * per : (place + 1) * per]
            out_ref[(mine ^ mask) * (size // groups) + block, r, pl.ds(pair * per, per), :] = part

    for n in range(len(labels)):
        first = 0
        for ref in done[n :: len(labels)]:
            for r in range(ref.shape[0]):
                keep(n, first + r, ref[r])
            first += ref.shape[0]
        cols, weight_ref = sets[n]
        score_pieces(pieces, cols, weight_ref, per, slots, lambda t, best: keep(n, first + t, best))


def finish_step(pieces, sets, done, labels, size, groups, per, slots):
    count = len(pieces) * per + sum(part.shape[0] for part in done[:: len(labels)])
    operands = [*pieces, *[part for both in sets for part in both], *done]
    return pl.pallas_call(
        functools.partial(finish_kernel, size, groups, len(pieces), per, slots, labels),
        out_shape=jax.ShapeDtypeStruct((size, count, 2 * per, slots), jnp.float32),
        in_specs=[VMEM] * len(operands),
        out_specs=VMEM,
        compiler_params=PARAMS,
        name="finish",
    )(*operands)


def gather_kernel(size, groups, rows, parts, best_ref, chamfer_ref):
    slots = best_ref.shape[2]
    per = parts.shape[2] // 2
    first = lax.axis_index("dev") % (size // groups) * groups
    tile = lax.broadcasted_iota(jnp.int32, (1, slots), 1)
    lane = lax.broadcasted_iota(jnp.int32, (per, chamfer_ref.shape[1]), 1)
    means = [jnp.zeros((per, chamfer_ref.shape[1]), jnp.float32)] * groups
    for k in range(groups):
        for r, (mask, s) in enumerate(rows):
            a = ((first + k) ^ mask) * per + s
            part = parts[first + k, r]
            kept = jnp.where(tile < USED, part, 0.0)
            for pair in range(2):
                e = k ^ (2 * pair)
                best_ref[a, pl.ds(e * per, per), :] = kept[pair * per : (pair + 1) * per]
                mean = part[pair * per : (pair + 1) * per, slots - 1 :]
                means[e] = jnp.where(lane == a, mean, means[e])
    for e in range(groups):
        chamfer_ref[pl.ds(e * per, per), :] = means[e]


def gather_results(parts, rows, size, groups):
    _, count, wide, slots = parts.shape
    return pl.pallas_call(
        functools.partial(gather_kernel, size, groups, rows),
        out_shape=(
            jax.ShapeDtypeStruct((2 * count, groups * wide // 2, slots), jnp.float32),
            jax.ShapeDtypeStruct((groups * wide // 2, 2 * count), jnp.float32),
        ),
        in_specs=[VMEM],
        out_specs=(VMEM, VMEM),
        compiler_params=PARAMS,
        name="gather_results",
    )(parts)


def flip(value, axis, mask):
    return lax.ppermute(value, axis, [(i, i ^ mask) for i in range(lax.axis_size(axis))])


def relay_kernel(in_ref, out_ref):
    out_ref[...] = in_ref[...]


def relay(block):
    return pl.pallas_call(
        relay_kernel,
        out_shape=jax.ShapeDtypeStruct(block.shape, block.dtype),
        in_specs=[VMEM],
        out_specs=VMEM,
        compiler_params=PARAMS,
        name="relay",
    )(block)


def split_kernel(in_ref, *outs):
    start = 0
    for out_ref in outs:
        out_ref[...] = in_ref[pl.ds(start, out_ref.shape[0]), :]
        start += out_ref.shape[0]


def split_block(block, count):
    rows, width = block.shape
    return pl.pallas_call(
        split_kernel,
        out_shape=[jax.ShapeDtypeStruct((size, width), block.dtype) for size in part_sizes(rows, count)],
        in_specs=[VMEM],
        out_specs=[VMEM] * count,
        compiler_params=PARAMS,
        name="split_block",
    )(block)


def on_device(features, tile_counts, projection):
    size, groups = lax.axis_size("dev"), lax.axis_size("grp")
    slots = features.shape[1]
    whole, halves = embed_tiles(features, tile_counts, projection)
    per = features.shape[0]
    opposite, across, beside = flip(whole, "dev", 4), flip(whole, "dev", 1), flip(whole, "dev", 2)
    labels, columns = [(0, 0, 0), (0, 1, 0)], [whole, beside]
    bit = groups // 2
    while bit > 1:
        columns += [flip(block, "grp", bit) for block in columns]
        labels += [(mask ^ bit, pair, 0) for mask, pair, _ in labels]
        bit //= 2
    cut = [2, 2, 2, 3]
    cut = [[whole]] + [split_block(block, count) for block, count in zip(columns[1:], cut[1:] + [2] * len(columns))]
    swapped = [[flip(part, "grp", 1) for part in cut[n]] for n in range(2)]
    rows = [(whole, 0), (across, 1), (opposite, 4), (flip(opposite, "dev", 1), 5)]
    bit = 8
    while bit < size:
        rows += [(flip(block, "dev", bit), mask ^ bit) for block, mask in rows]
        bit *= 2
    early, late = [block for block, _ in rows[:-1]], [block for block, _ in rows[-1:]]

    def column_set(which):
        blocks, names = [columns[n] for n in which], [labels[n] for n in which]
        for n in which:
            mask, pair, _ = labels[n]
            since = 0
            for part in swapped[n]:
                blocks.append(part)
                names.append((mask ^ 1, pair, since))
                since += part.shape[0]
        return blocks, tuple(names)

    near, near_names = column_set(range(2))
    *near_set, scored = first_step(early[:3], near, near_names, per, slots)
    scored, cut[-1] = lax.optimization_barrier((scored, cut[-1]))
    swapped += [[flip(part, "grp", 1) for part in parts] for parts in cut[2:]]
    far, far_names = column_set(range(2, len(columns)))
    *far_set, rest = first_step(early[:3], far, far_names, per, slots)
    sets, done = [near_set, far_set], [scored, rest]
    for i in range(3, len(early), 3):
        done += [score_step(early[i : i + 3], *both, per, slots) for both in sets]
    places = [tuple(dict.fromkeys((mask, pair) for mask, pair, _ in names)) for names in (near_names, far_names)]
    results = finish_step(late, sets, done, places, size, groups, per, slots)
    parts = lax.all_to_all(results, "dev", split_axis=0, concat_axis=0, tiled=True)
    names = tuple((mask, s) for _, mask in rows for s in range(per))
    best, chamfer = gather_results(parts, names, size, groups)
    return best, chamfer.T


def solution(mesh):
    return jax.shard_map(
        on_device,
        mesh=mesh,
        in_specs=(P(("grp", "dev"), None, None), P(("grp", "dev")), P()),
        out_specs=(P("grp", "dev", None), P("grp", "dev")),
        check_vma=False,
    )
```
